128 devices in a mesh: row: 8 (over z, core), col: 16 (over y, x).
Axes of the slice: x: 4, y: 4, z: 4, core: 2. Of those that a mesh axis runs over, the one named last changes fastest.
Arguments:
- features: float32 [2048, 4, 9, 1920], P(('row', 'col')), may hold values from -12 to 12, as said below
- query_row: int32 [8192], P(('row', 'col')), may hold values from 0 to 15
- target_device: int32 [8192, 1], P(('row', 'col')), may hold values from 0 to 127; in each aligned block of 64 rows (0 to 63, 64 to 127, ...) no two rows name the same one
- target_row: int32 [8192], P(('row', 'col')), may hold values from 0 to 15
- pair_count: int32 [128], P(('row', 'col')), may hold values from 1 to 64, 6144 in all
- conv_first: bfloat16 [9, 32], replicated, may hold values from -2 to 2
- conv_second: bfloat16 [288, 64], replicated, may hold values from -0.5 to 0.5
- conv_third: bfloat16 [576, 128], replicated, may hold values from -0.375 to 0.375
- conv_last: bfloat16 [1152, 1], replicated, may hold values from -0.25 to 0.25
Outputs:
- maps: float32 [8192, 16], P(('row', 'col'))
- scores: float32 [8192], P(('row', 'col'))
The draws below stay inside these ranges and needn't reach their ends.
Inputs may be any that keep to these rules, and one draw needn't show every extreme that they name: Region features are finite values of order one. `target_device`: among the 64 slots of one device, at most 1 name one target device; this is reached.
All inputs are finite; a program needn't handle non-finite values. No bound on the sum of `pair_count` on one device may be relied on, other than what follows from the above.
Results may differ from the reference program's by a relative error of at most 0.004.
Values may be sent and summed in bfloat16 or wider, within the bound.
A program may use at most 128 MiB of HBM per device.

```python
import math
import jax
import jax.numpy as jnp
import numpy as np
from jax import lax

DIM = 1920
REGIONS = 9
FRAMES = 4
CH1 = 32
CH2 = 64
CH3 = 128
CAPACITY = 1
CLIPS_DEV = 16
PAIRS_DEV = 64
CLIPS = 2048
PAIRS = 8192
N_ROW = 8
N_COL = 16


def shared_regions(key):
    return jax.random.normal(jax.random.fold_in(key, 5), (1, 1, REGIONS, DIM), jnp.float32)


def draw_features(key, part):
    common = shared_regions(key)
    key = jax.random.fold_in(key, 11)
    weight_key, noise_key = jax.random.split(key, 2)
    weights = jax.random.uniform(weight_key, (CLIPS, FRAMES, REGIONS, 1), jnp.float32, 0.0, 2.0)
    noise = jax.random.normal(noise_key, (CLIPS, FRAMES, REGIONS, DIM), jnp.float32)
    values = weights * common + noise
    return jnp.clip(values, -12.0, 12.0)


def plant(array, stream_key, smallest, top_value):
    extent = array.shape
    index_at = [jax.random.randint(jax.random.fold_in(stream_key, axis), (), 0, extent[axis]) for axis in range(len(extent))]
    array = array.at[tuple(index_at)].set(smallest)
    longest = extent.index(max(extent))
    index_at[longest] = (index_at[longest] + 1) % extent[longest]
    return array.at[tuple(index_at)].set(top_value)


def profile(number_of, total, limit, slope):
    loads = [(1 << 20) // math.isqrt(standing ** slope) + 1 for standing in range(2, number_of + 1)]
    spare, given = total - limit - (number_of - 1), [1] * (number_of - 1)
    while spare > 0:
        movable = [i for i in range(number_of - 1) if given[i] < limit]
        mass, remaining = sum([loads[i] for i in movable]), spare
        for i in movable:
            more = min(limit - given[i], max(1, remaining * loads[i] // mass), spare)
            given[i] = given[i] + more
            spare = spare - more
    return np.array([limit] + given)


def uneven_parts(key, amount, total, bound, lean):
    if amount == 2:
        one = jax.random.randint(key, (), max(1, total - bound), min(bound, total - 1) + 1)
        return jnp.stack([one, total - one])
    sizes = jnp.asarray(profile(amount, total, bound, lean), jnp.int32)
    couples = (amount - 1) // 2
    source_of, taker = sizes[1:1 + 2 * couples:2], sizes[2:2 + 2 * couples:2]
    room = jnp.minimum(source_of - 1, bound - taker)
    passed = jax.random.randint(jax.random.fold_in(key, 1), (couples,), 0, 1 << 20) % (room + 1)
    sizes = sizes.at[1:1 + 2 * couples:2].set(source_of - passed).at[2:2 + 2 * couples:2].set(taker + passed)
    return sizes[jax.random.permutation(jax.random.fold_in(key, 2), amount)]


def deal_out(own_key, own, number, rows, amount, top, limit, lean):
    ranking = jax.random.permutation(own_key, amount)
    heavy_load, usual = shares(amount, rows * top, limit, lean, True), shares(amount, rows * top, limit, lean, False)
    places = jnp.arange(amount)

    def named(tallies, offset_by):
        used = int((tallies > 0).sum())
        fixed = max(1, used // 4)
        moved = fixed + (places - fixed + offset_by * (used - fixed)) % max(1, amount - fixed)
        return jnp.zeros((amount,), jnp.int32).at[ranking[jnp.where(places < fixed, places, moved)]].set(jnp.asarray(tallies, jnp.int32))

    tallies = jnp.where(number % 4 == 0, named(heavy_load, number // 4), named(usual, number - number // 4 - 1))
    mixed = jax.random.permutation(jax.random.fold_in(own, 3), amount)
    donor, receiver = mixed[0:amount // 2 * 2:2], mixed[1:amount // 2 * 2:2]
    slack = jnp.minimum(tallies[donor] - 1, limit - tallies[receiver]) // 2
    slack = jnp.where((donor == ranking[0]) | (receiver == ranking[0]) | (tallies[receiver] == 0), 0, jnp.maximum(slack, 0))
    moved = jax.random.randint(jax.random.fold_in(own, 4), (amount // 2,), 0, 1 << 20) % (slack + 1)
    tallies = tallies.at[donor].add(-moved).at[receiver].add(moved)
    members = jnp.searchsorted(jnp.cumsum(tallies), jnp.arange(rows * top), side="right").astype(jnp.int32)
    table = members.reshape(top, rows).T
    table = table[jax.random.permutation(jax.random.fold_in(own, 1), rows)]
    offset_by = jax.random.randint(jax.random.fold_in(own, 2), (rows, 1), 0, top)
    return jnp.take_along_axis(table, (jnp.arange(top)[None, :] + offset_by) % top, axis=1)


def shares(count, total, reach, skew, full):
    loads = [(1 << 20) // math.isqrt(standing ** skew) + 1 for standing in range(1, count + 1)]
    largest = reach if full else min(reach, max(-(-total // count), total * loads[0] // sum(loads)))
    least = 1 if total - largest >= count - 1 else 0
    given, rest = [largest] + [least] * (count - 1), total - largest - least * (count - 1)
    while rest > 0:
        candidates = [i for i in range(1, count) if given[i] < largest] or [i for i in range(1, count) if given[i] < reach]
        pool, budget = sum([loads[i] for i in candidates]), rest
        for i in candidates:
            addition = min(reach - given[i], max(1, budget * loads[i] // pool), rest)
            given[i] = given[i] + addition
            rest = rest - addition
    return np.array(given)


def centred(own_key, dims, deviation, bound, kind=jnp.bfloat16):
    array = deviation * jax.random.normal(own_key, dims, jnp.float32)
    return jnp.clip(array, min=-bound, max=bound).astype(kind)


def setup_inputs(seed: int = 0) -> dict:
    streams_of = jax.random.split(jax.random.key(seed), 10)
    features = draw_features(jax.random.fold_in(streams_of[9], 71), 0)
    query_row = plant(jax.random.randint(streams_of[1], (PAIRS,), 0, CLIPS_DEV), jax.random.fold_in(streams_of[1], 1), 0, CLIPS_DEV - 1).astype(jnp.int32)
    target_device_keys = jax.random.split(jax.random.fold_in(streams_of[2], 1), PAIRS // PAIRS_DEV)
    target_device_turns = jax.random.permutation(jax.random.fold_in(streams_of[2], 3), PAIRS // PAIRS_DEV)
    target_device = jax.vmap(lambda own, number: deal_out(jax.random.fold_in(streams_of[2], 2), own, number, PAIRS_DEV, N_ROW * N_COL, 1, CAPACITY, 2))(target_device_keys, target_device_turns).reshape((PAIRS, 1))
    target_row = plant(jax.random.randint(streams_of[3], (PAIRS,), 0, CLIPS_DEV), jax.random.fold_in(streams_of[3], 1), 0, CLIPS_DEV - 1).astype(jnp.int32)
    pair_count = uneven_parts(streams_of[4], N_ROW * N_COL, 3 * PAIRS // 4, PAIRS_DEV, 2).astype(jnp.int32)
    conv_first = centred(streams_of[5], (9, CH1), 9 ** -0.5, 2.0)
    conv_second = centred(streams_of[6], (9 * CH1, CH2), (9 * CH1 // 2) ** -0.5, 0.5)
    conv_third = centred(streams_of[7], (9 * CH2, CH3), (9 * CH2 // 2) ** -0.5, 0.375)
    conv_last = centred(streams_of[8], (9 * CH3, 1), (9 * CH3 // 2) ** -0.5, 0.25)
    return dict(features=features, query_row=query_row, target_device=target_device, target_row=target_row, pair_count=pair_count, conv_first=conv_first, conv_second=conv_second, conv_third=conv_third, conv_last=conv_last)


def unit_rows(block):
    scale = 1.0 / jnp.sqrt(lax.optimization_barrier(jnp.sum(block * block, axis=-1, keepdims=True)) + 1e-06)
    return (block * scale).astype(jnp.bfloat16)

def convolve(activations, kernel):
    frames = activations.shape[1]
    channels = activations.shape[3]
    padded = jnp.pad(activations, ((0, 0), (1, 1), (1, 1), (0, 0)))
    wide = jnp.concatenate([padded[:, :, shift:shift + frames, :] for shift in range(3)], axis=-1)
    parts = kernel.astype(jnp.float32).reshape(3, 3 * channels, kernel.shape[1])
    total = jnp.zeros((activations.shape[0], frames, frames, kernel.shape[1]), jnp.float32)
    for shift in range(3):
        total = total + jnp.einsum('bijc,co->bijo', wide[:, shift:shift + frames], parts[shift], precision=lax.Precision.HIGHEST)
    return total

def compare_pairs(left, right, kernels):
    batch = left.shape[0]
    similarity = jnp.einsum('bxd,byd->bxy', left.astype(jnp.float32), right.astype(jnp.float32), precision=lax.Precision.HIGHEST)
    similarity = similarity.reshape(batch, FRAMES, REGIONS, FRAMES, REGIONS)
    frame_sim = lax.optimization_barrier(jnp.mean(lax.optimization_barrier(jnp.max(similarity, axis=4)), axis=2))
    hidden = frame_sim[..., None]
    for kernel in kernels[:3]:
        hidden = jax.nn.relu(convolve(hidden, kernel))
    final = convolve(hidden, kernels[3])[..., 0]
    return jnp.clip(final, -1.0, 1.0).reshape(batch, FRAMES * FRAMES)

def reference(features, query_row, target_device, target_row, pair_count, conv_first, conv_second, conv_third, conv_last):
    kernels = (conv_first, conv_second, conv_third, conv_last)
    positions = jnp.arange(PAIRS, dtype=jnp.int32)
    owner_device = positions // PAIRS_DEV
    is_live = positions % PAIRS_DEV < pair_count[owner_device]
    query_clip = owner_device * CLIPS_DEV + query_row
    target_clip = target_device[:, 0] * CLIPS_DEV + target_row

    def one_group(indices):
        query_ids, target_ids = indices
        left = unit_rows(features[query_ids]).reshape(query_ids.shape[0], FRAMES * REGIONS, DIM)
        right = unit_rows(features[target_ids]).reshape(target_ids.shape[0], FRAMES * REGIONS, DIM)
        return compare_pairs(left, right, kernels)
    groups = PAIRS // 16
    refined = lax.map(one_group, (query_clip.reshape(groups, 16), target_clip.reshape(groups, 16)))
    refined = refined.reshape(PAIRS, FRAMES * FRAMES)
    maps = jnp.where(is_live[:, None], refined, jnp.float32(0.0))
    scores = lax.optimization_barrier(jnp.mean(lax.optimization_barrier(jnp.max(maps.reshape(PAIRS, FRAMES, FRAMES), axis=2)), axis=1))
    return (maps, scores)
```

```python
import functools

import jax
import jax.numpy as jnp
from jax import lax
from jax.experimental import pallas as pl
from jax.experimental.pallas import tpu as pltpu
from jax.sharding import PartitionSpec as P

MESH = pl.DeviceIdType.MESH
CLIPS = 16
FRAMES = 4
REGIONS = 9
DIM = 1920
LANES = 128
SLICES = DIM // LANES
COLS = 16
ROWS = 8
MAIN = 32
TAILS = CLIPS * MAIN
BLOCK = CLIPS * FRAMES * REGIONS
SLOTS = 64
HALVES = 22
GROUPS = HALVES // 2
GROUP_ROWS = 2 * 40
PAY = GROUPS * GROUP_ROWS
VMEM_LIMIT = 60 * 2**20


def gather_kernel(
    feat, idx, table, idx_all, units, scales, a_send, a_recv, i_send, i_recv, b_send, b_recv, own_sem
):
    row = lax.axis_index("row")
    me = lax.axis_index("col")
    z = row // 2
    core = lax.rem(row, 2)
    rows_z = lambda step: lax.rem(z + step, 4) * 2 + core
    rows_mate = lambda step: lax.rem(z + step, 4) * 2 + 1 - core
    mate = z * 2 + 1 - core

    barrier = pltpu.get_barrier_semaphore()

    def greet(i, carry):
        pl.semaphore_signal(
            barrier, inc=1, device_id=(row, lax.rem(me + i, COLS)), device_id_type=MESH
        )
        return carry

    lax.fori_loop(1, COLS, greet, 0)
    for other in (rows_z(1), rows_z(2), rows_z(3), mate):
        pl.semaphore_signal(barrier, inc=1, device_id=(other, me), device_id_type=MESH)

    def measure(i, carry):
        c = i // FRAMES
        f = lax.rem(i, FRAMES)
        x = feat[c, f]
        total = jnp.sum(x * x, axis=-1, keepdims=True)
        scales[c, f] = jnp.broadcast_to(1.0 / jnp.sqrt(total + 1e-06), (REGIONS, LANES))
        return carry

    lax.fori_loop(0, CLIPS * FRAMES, measure, 0)
    pl.semaphore_wait(barrier, COLS - 1 + 4)

    def idx_copy(i):
        return pltpu.make_async_remote_copy(
            src_ref=idx,
            dst_ref=idx_all.at[me],
            send_sem=i_send.at[i],
            recv_sem=i_recv.at[i],
            device_id=(row, lax.rem(me + i, COLS)),
            device_id_type=MESH,
        )

    def slice_copy(i):
        n = lax.rem(me + i, COLS)
        return pltpu.make_async_remote_copy(
            src_ref=units.at[n],
            dst_ref=table.at[row, me],
            send_sem=a_send.at[i],
            recv_sem=a_recv.at[i],
            device_id=(row, n),
            device_id_type=MESH,
        )

    def arrival(i, s):
        return pltpu.make_async_remote_copy(
            src_ref=units.at[0],
            dst_ref=table.at[row, s],
            send_sem=a_send.at[i],
            recv_sem=a_recv.at[i],
            device_id=(row, s),
            device_id_type=MESH,
        )

    def fill(n):
        lanes = pl.ds(pl.multiple_of(n * LANES, LANES), LANES)

        def quad(j, carry):
            tails = []
            for k in range(4):
                c = j * 4 + k
                parts = [feat[c, f, :, lanes] * scales[c, f] for f in range(FRAMES)]
                main = jnp.concatenate([p[:8] for p in parts], axis=0)
                units[n, pl.ds(pl.multiple_of(c * MAIN, MAIN), MAIN), :] = main.astype(jnp.bfloat16)
                tails += [p[8:9] for p in parts]
            tail = jnp.concatenate(tails, axis=0)
            units[n, pl.ds(pl.multiple_of(TAILS + j * 16, 16), 16), :] = tail.astype(jnp.bfloat16)
            return carry

        lax.fori_loop(0, CLIPS // 4, quad, 0)

    own_idx = pltpu.make_async_copy(idx, idx_all.at[me], own_sem.at[1])
    own_idx.start()

    def send_idx(i, carry):
        idx_copy(i).start()
        return carry

    lax.fori_loop(1, COLS, send_idx, 0)

    own = pltpu.make_async_copy(units.at[me], table.at[row, me], own_sem.at[0])

    @pl.when(me < SLICES)
    def _():
        fill(me)
        own.start()

    def send_slice(i, carry):
        n = lax.rem(me + i, COLS)

        @pl.when(n < SLICES)
        def _():
            fill(n)
            slice_copy(i).start()

        return carry

    lax.fori_loop(1, COLS, send_slice, 0)

    def forward(source_row, s, target_row, kind, j):
        return pltpu.make_async_remote_copy(
            src_ref=table.at[source_row, s],
            dst_ref=table.at[source_row, s],
            send_sem=b_send.at[kind, j],
            recv_sem=b_recv.at[kind, j],
            device_id=(target_row, me),
            device_id_type=MESH,
        )

    @pl.when(me < SLICES)
    def _():
        own.wait()

        def spread(j, carry):
            s = lax.rem(me - j + COLS, COLS)

            @pl.when(j > 0)
            def _():
                arrival(j, s).wait_recv()

            for step in (1, 3, 2):
                forward(row, s, rows_z(step), step, j).start()
            forward(row, s, mate, 4, j).start()
            return carry

        lax.fori_loop(0, COLS, spread, 0)

        def relay(j, carry):
            s = lax.rem(me - j + COLS, COLS)
            for step in (1, 3, 2):
                forward(rows_z(4 - step), s, rows_z(step), step, j).wait_recv()
                forward(rows_z(4 - step), s, mate, 4 + step, j).start()
            return carry

        lax.fori_loop(0, COLS, relay, 0)

        def finish(j, carry):
            s = lax.rem(me - j + COLS, COLS)
            forward(rows_mate(0), s, mate, 4, j).wait_recv()
            forward(row, s, mate, 4, j).wait_send()
            for step in (1, 3, 2):
                forward(rows_mate(4 - step), s, mate, 4 + step, j).wait_recv()
                forward(rows_z(4 - step), s, mate, 4 + step, j).wait_send()
                forward(row, s, rows_z(step), step, j).wait_send()
            return carry

        lax.fori_loop(0, COLS, finish, 0)

    own_idx.wait()

    def drain(i, carry):
        idx_copy(i).wait()

        @pl.when(lax.rem(me + i, COLS) < SLICES)
        def _():
            slice_copy(i).wait_send()

        return carry

    lax.fori_loop(1, COLS, drain, 0)


def gather(features, packed):
    dma = pltpu.SemaphoreType.DMA
    return pl.pallas_call(
        gather_kernel,
        out_shape=(
            jax.ShapeDtypeStruct((ROWS, COLS, BLOCK, LANES), jnp.bfloat16),
            jax.ShapeDtypeStruct((COLS, 8, LANES), jnp.int32),
        ),
        in_specs=[pl.BlockSpec(memory_space=pltpu.VMEM)] * 2,
        out_specs=[pl.BlockSpec(memory_space=pl.ANY)] * 2,
        scratch_shapes=[
            pltpu.VMEM((SLICES, BLOCK, LANES), jnp.bfloat16),
            pltpu.VMEM((CLIPS, FRAMES, REGIONS, LANES), jnp.float32),
            dma((COLS,)),
            dma((COLS,)),
            dma((COLS,)),
            dma((COLS,)),
            dma((8, COLS)),
            dma((8, COLS)),
            dma((2,)),
        ],
        compiler_params=pltpu.CompilerParams(
            collective_id=0, has_side_effects=True, vmem_limit_bytes=VMEM_LIMIT
        ),
    )(features, packed)


def compare_kernel(idx, table, pay, tails, products):
    row = lax.axis_index("row")
    me = lax.axis_index("col")

    @pl.when(me < SLICES)
    def _():
        def widen(i, carry):
            r = i // COLS
            s = lax.rem(i, COLS)
            tails[pl.ds(pl.multiple_of(i * 64, 64), 64), :] = table[
                r, s, TAILS : TAILS + 64, :
            ].astype(jnp.float32)
            return carry

        lax.fori_loop(0, ROWS * COLS, widen, 0)
        sub = lax.broadcasted_iota(jnp.int32, (8, LANES), 0)
        lane = lax.broadcasted_iota(jnp.int32, (8, LANES), 1)
        block = lax.rem(lane // MAIN, 4)
        third = lax.rem(lane, 8)
        choice = jnp.where(block < 3, block, third)

        def pick(parts):
            return jnp.where(choice == 0, parts[0], jnp.where(choice == 1, parts[1], parts[2]))

        def group(i, carry):
            n = i // GROUPS
            g = lax.rem(i, GROUPS)
            halves = []
            queries = []
            for b in range(2):
                main = []
                rows = []
                asked = []
                for t in range(3):
                    slot = jnp.minimum(t * HALVES + g * 2 + b, SLOTS - 1)
                    word = idx[n, 0, slot]
                    asked.append(word & 15)
                    clip = (word >> 4) & 15
                    device = word >> 8
                    start = pl.multiple_of(clip * MAIN, MAIN)
                    main.append(table[device >> 4, device & 15, pl.ds(start, MAIN), :])
                    rows.append((device * CLIPS + clip) * FRAMES)
                tail = []
                for f in range(FRAMES):
                    got = [
                        jnp.broadcast_to(tails[pl.ds(rows[t] + f, 1), :], (8, LANES))
                        for t in range(3)
                    ]
                    tail.append(jnp.where(sub == 0, got[0], jnp.where(sub == 1, got[1], got[2])))
                halves += main + [jnp.concatenate(tail, axis=0).astype(jnp.bfloat16)]
                queries.append(asked)
            targets = jnp.concatenate(halves, axis=0)
            products[...] = lax.dot_general(
                table[row, n],
                targets,
                (((1,), (1,)), ((), ())),
                preferred_element_type=jnp.float32,
            )
            ends = []
            for b in range(2):
                cols = slice(b * LANES, (b + 1) * LANES)
                for f in range(FRAMES):
                    parts = [
                        products[pl.ds(pl.multiple_of(q * MAIN + f * 8, 8), 8), cols]
                        for q in queries[b]
                    ]
                    ends.append((b, f, pick(parts)))
            base = pl.multiple_of(g * GROUP_ROWS, 16)
            for b in range(2):
                kept = [v for bb, f, v in ends if bb == b]
                pay[n, pl.ds(base + b * MAIN, MAIN), :] = jnp.concatenate(kept, axis=0).astype(
                    jnp.bfloat16
                )
            last = []
            for b in range(2):
                cols = slice(b * LANES, (b + 1) * LANES)
                parts = []
                for q in queries[b]:
                    pair = products[pl.ds(pl.multiple_of(TAILS + (q >> 1) * 8, 8), 8), cols]
                    parts.append(jnp.where((q & 1) == 0, pair, pltpu.roll(pair, 4, 0)))
                last.append(pick(parts))
            pay[n, pl.ds(base + 2 * MAIN, 16), :] = jnp.concatenate(last, axis=0).astype(
                jnp.bfloat16
            )
            return carry

        lax.fori_loop(0, COLS * GROUPS, group, 0)


def compare(idx_all, table):
    return pl.pallas_call(
        compare_kernel,
        out_shape=jax.ShapeDtypeStruct((COLS, PAY, LANES), jnp.bfloat16),
        in_specs=[
            pl.BlockSpec(memory_space=pltpu.SMEM),
            pl.BlockSpec(memory_space=pltpu.VMEM),
        ],
        out_specs=pl.BlockSpec(memory_space=pltpu.VMEM),
        scratch_shapes=[
            pltpu.VMEM((ROWS * COLS * CLIPS * FRAMES, LANES), jnp.float32),
            pltpu.VMEM((BLOCK, 2 * LANES), jnp.float32),
        ],
        compiler_params=pltpu.CompilerParams(vmem_limit_bytes=VMEM_LIMIT),
    )(idx_all, table)


def return_kernel(pay, got, send, recv, own_sem):
    row = lax.axis_index("row")
    me = lax.axis_index("col")
    barrier = pltpu.get_barrier_semaphore()

    def greet(i, carry):
        pl.semaphore_signal(
            barrier, inc=1, device_id=(row, lax.rem(me + i, COLS)), device_id_type=MESH
        )
        return carry

    lax.fori_loop(1, COLS, greet, 0)
    pl.semaphore_wait(barrier, COLS - 1)

    def copy(i):
        n = lax.rem(me + i, COLS)
        return pltpu.make_async_remote_copy(
            src_ref=pay.at[n],
            dst_ref=got.at[me],
            send_sem=send.at[i],
            recv_sem=recv.at[i],
            device_id=(row, n),
            device_id_type=MESH,
        )

    own = pltpu.make_async_copy(pay.at[me], got.at[me], own_sem)

    @pl.when(me < SLICES)
    def _():
        own.start()

        def start(i, carry):
            copy(i).start()
            return carry

        lax.fori_loop(1, COLS, start, 0)

    def arrive(i, carry):
        @pl.when(lax.rem(me - i + COLS, COLS) < SLICES)
        def _():
            copy(i).wait_recv()

        return carry

    lax.fori_loop(1, COLS, arrive, 0)

    @pl.when(me < SLICES)
    def _():
        own.wait()

        def drain(i, carry):
            copy(i).wait_send()
            return carry

        lax.fori_loop(1, COLS, drain, 0)


def return_pay(pay):
    dma = pltpu.SemaphoreType.DMA
    return pl.pallas_call(
        return_kernel,
        out_shape=jax.ShapeDtypeStruct(pay.shape, pay.dtype),
        in_specs=[pl.BlockSpec(memory_space=pl.ANY)],
        out_specs=pl.BlockSpec(memory_space=pl.ANY),
        scratch_shapes=[dma((COLS,)), dma((COLS,)), dma],
        compiler_params=pltpu.CompilerParams(collective_id=1, has_side_effects=True),
    )(pay)


def split(x):
    high = x.astype(jnp.bfloat16)
    return high, (x - high.astype(jnp.float32)).astype(jnp.bfloat16)


def dot_split(x, kernel):
    high, low = split(x)
    return jnp.dot(high, kernel, preferred_element_type=jnp.float32) + jnp.dot(
        low, kernel, preferred_element_type=jnp.float32
    )


def convolve(padded, kernel):
    channels = padded.shape[3]
    rows = padded.shape[2]
    total = None
    for dy in range(3):
        wide = jnp.concatenate(
            [padded[dy : dy + 4, dx : dx + 4] for dx in range(3)], axis=-1
        ).reshape(16 * rows, 3 * channels)
        part = dot_split(wide, kernel[dy * 3 * channels : (dy + 1) * 3 * channels, :])
        total = part if total is None else total + part
    return total


def finish_kernel(count, got, first, second, third, last, maps, scores, frames, one, two):
    lane = lax.broadcasted_iota(jnp.int32, (8, LANES), 1)
    shift = lambda x, by: pltpu.roll(x, (LANES - by) % LANES, 1)
    frames[...] = jnp.zeros_like(frames)

    def best(x):
        top = jnp.maximum(x, shift(x, 1))
        top = jnp.maximum(top, shift(top, 2))
        top = jnp.maximum(top, shift(top, 4))
        ends = [shift(x, 96 + t - 32 * t) for t in range(3)]
        end = jnp.where(lane < 32, ends[0], jnp.where(lane < 64, ends[1], ends[2]))
        return jnp.maximum(top, end)

    def group(g, carry):
        base = pl.multiple_of(g * GROUP_ROWS, 16)
        total = jnp.zeros((GROUP_ROWS, LANES), jnp.float32)
        for m in range(SLICES):
            total += got[m, pl.ds(base, GROUP_ROWS), :].astype(jnp.float32)
        for b in range(2):
            tail = best(total[2 * MAIN + b * 8 : 2 * MAIN + b * 8 + 8])
            for f in range(FRAMES):
                start = b * MAIN + f * 8
                main = jnp.sum(best(total[start : start + 8]), axis=0, keepdims=True)
                frames[f, pl.ds(g * 2 + b, 1), :] = (main + tail[f : f + 1]) * (1.0 / REGIONS)
        return carry

    lax.fori_loop(0, GROUPS, group, 0)

    pairs = 72
    one[...] = jnp.zeros_like(one)
    two[...] = jnp.zeros_like(two)
    ch1 = first.shape[1]
    ch2 = second.shape[1]
    ch3 = third.shape[1]
    taps = first[...].astype(jnp.float32)
    spread = []
    for i in range(FRAMES):
        value = frames[i]
        for j in range(FRAMES):
            spread.append(
                jnp.concatenate(
                    [
                        jnp.broadcast_to(
                            value[:, 32 * t + 8 * j : 32 * t + 8 * j + 1], (24, ch1)
                        )
                        for t in range(3)
                    ],
                    axis=0,
                )
            )
    around = lambda i, j: [
        (dy * 3 + dx, (i + dy - 1) * 4 + j + dx - 1)
        for dy in range(3)
        for dx in range(3)
        if 0 <= i + dy - 1 < 4 and 0 <= j + dx - 1 < 4
    ]
    for i in range(FRAMES):
        for j in range(FRAMES):
            total = jnp.zeros((pairs, ch1), jnp.float32)
            for tap, pos in around(i, j):
                total += spread[pos] * taps[tap : tap + 1, :]
            one[1 + i, 1 + j] = jnp.maximum(total, 0.0)
    hidden = jnp.maximum(convolve(one, second), 0.0)
    two[1:5, 1:5] = hidden.reshape(4, 4, pairs, ch2)
    hidden = jnp.maximum(convolve(two, third), 0.0)
    high, low = split(hidden)
    nt = (((1,), (1,)), ((), ()))
    response = lax.dot_general(
        high, last[...], nt, preferred_element_type=jnp.float32
    ) + lax.dot_general(low, last[...], nt, preferred_element_type=jnp.float32)
    response = response.reshape(16, pairs, response.shape[1])
    tap_lane = lax.broadcasted_iota(jnp.int32, (pairs, response.shape[2]), 1)
    out_lane = lax.broadcasted_iota(jnp.int32, (pairs, LANES), 1)
    result = jnp.zeros((pairs, LANES), jnp.float32)
    for i in range(FRAMES):
        for j in range(FRAMES):
            total = jnp.zeros((pairs, response.shape[2]), jnp.float32)
            for tap, pos in around(i, j):
                total += jnp.where(tap_lane == tap, response[pos], 0.0)
            value = jnp.sum(total, axis=1, keepdims=True)
            result = jnp.where(out_lane == i * 4 + j, value, result)
    line = lax.broadcasted_iota(jnp.int32, (pairs, LANES), 0)
    slot = (line // 24) * HALVES + lax.rem(line, 24)
    result = jnp.where(slot < count[0], jnp.clip(result, -1.0, 1.0), 0.0)
    top = jnp.maximum(result, shift(result, 1))
    top = jnp.maximum(top, shift(top, 2))
    kept = (out_lane < 16) & (lax.rem(out_lane, 4) == 0)
    score = jnp.sum(jnp.where(kept, top, 0.0), axis=1, keepdims=True) * (1.0 / FRAMES)
    for t in range(3):
        amount = min(HALVES, SLOTS - t * HALVES)
        maps[t * HALVES : t * HALVES + amount, :] = result[t * 24 : t * 24 + amount, :16]
        scores[t * HALVES : t * HALVES + amount, :] = score[t * 24 : t * 24 + amount]


def finish(count, got, first, second, third, last):
    vmem = pl.BlockSpec(memory_space=pltpu.VMEM)
    return pl.pallas_call(
        finish_kernel,
        out_shape=(
            jax.ShapeDtypeStruct((SLOTS, FRAMES * FRAMES), jnp.float32),
            jax.ShapeDtypeStruct((SLOTS, 1), jnp.float32),
        ),
        in_specs=[pl.BlockSpec(memory_space=pltpu.SMEM)] + [vmem] * 5,
        out_specs=[vmem] * 2,
        scratch_shapes=[
            pltpu.VMEM((FRAMES, 24, LANES), jnp.float32),
            pltpu.VMEM((6, 6, 72, first.shape[1]), jnp.float32),
            pltpu.VMEM((6, 6, 72, second.shape[1]), jnp.float32),
        ],
        compiler_params=pltpu.CompilerParams(vmem_limit_bytes=VMEM_LIMIT),
    )(count, got, first, second, third, last)


def per_device(
    features,
    query_row,
    target_device,
    target_row,
    pair_count,
    conv_first,
    conv_second,
    conv_third,
    conv_last,
):
    packed = query_row + (target_row << 4) + (target_device[:, 0] << 8)
    packed = jnp.broadcast_to(jnp.pad(packed, (0, LANES - SLOTS))[None], (8, LANES))
    table, idx_all = gather(features, packed)
    pay = compare(idx_all, table)
    got = return_pay(pay)
    last = conv_last.reshape(9, conv_third.shape[1])
    maps, scores = finish(pair_count, got, conv_first, conv_second, conv_third, last)
    return maps, scores[:, 0]


def solution(mesh):
    return jax.shard_map(
        per_device,
        mesh=mesh,
        in_specs=(
            P(("row", "col"), None, None, None),
            P(("row", "col")),
            P(("row", "col"), None),
            P(("row", "col")),
            P(("row", "col")),
            P(),
            P(),
            P(),
            P(),
        ),
        out_specs=(P(("row", "col"), None), P(("row", "col"))),
        check_vma=False,
    )
```

```python
import functools

import jax
import jax.numpy as jnp
from jax import lax
from jax.experimental import pallas as pl
from jax.experimental.pallas import tpu as pltpu
from jax.sharding import PartitionSpec as P

MESH = pl.DeviceIdType.MESH
CLIPS = 16
FRAMES = 4
REGIONS = 9
DIM = 1920
LANES = 128
SLICES = DIM // LANES
COLS = 16
ROWS = 8
MAIN = 32
TILES = CLIPS + CLIPS * FRAMES // MAIN
SLOTS = 64
HALVES = 22
GROUPS = HALVES // 2
GROUP_ROWS = 2 * 40
PAY = GROUPS * GROUP_ROWS
VMEM_LIMIT = 60 * 2**20


def split(x):
    high = x.astype(jnp.bfloat16)
    return high, (x - high.astype(jnp.float32)).astype(jnp.bfloat16)


def dot_split(x, kernel):
    high, low = split(x)
    return jnp.dot(high, kernel, preferred_element_type=jnp.float32) + jnp.dot(
        low, kernel, preferred_element_type=jnp.float32
    )


def around(i, j):
    return [
        (dy * 3 + dx, (i + dy - 1) * 4 + j + dx - 1)
        for dy in range(3)
        for dx in range(3)
        if 0 <= i + dy - 1 < 4 and 0 <= j + dx - 1 < 4
    ]


def shift(x, by):
    return pltpu.roll(x, (LANES - by) % LANES, 1)


def make_units(feat, scales, end_scales):
    def measure():
        def quad(j, carry):
            ends = []
            for k in range(4):
                c = j * 4 + k
                parts = []
                for r in range(REGIONS):
                    x = feat[c, r]
                    total = jnp.sum(x * x, axis=-1, keepdims=True)
                    parts.append(jnp.broadcast_to(1.0 / jnp.sqrt(total + 1e-06), (FRAMES, LANES)))
                scales[c] = jnp.concatenate(parts[:8], axis=0)
                ends.append(parts[8])
            end_scales[j] = jnp.concatenate(ends, axis=0)
            return carry

        lax.fori_loop(0, CLIPS // 4, quad, 0)

    def fill(block, n):
        lanes = pl.ds(pl.multiple_of(n * LANES, LANES), LANES)

        def quad(j, carry):
            ends = []
            for k in range(4):
                c = j * 4 + k
                parts = [feat[c, r, :, lanes] for r in range(REGIONS)]
                main = jnp.concatenate(parts[:8], axis=0) * scales[c]
                block[c] = main.astype(jnp.bfloat16)
                ends.append(parts[8])
            end = jnp.concatenate(ends, axis=0) * end_scales[j]
            place = pl.ds(pl.multiple_of(lax.rem(j, 2) * 16, 16), 16)
            block[CLIPS + j // 2, place, :] = end.astype(jnp.bfloat16)
            return carry

        lax.fori_loop(0, CLIPS // 4, quad, 0)

    return measure, fill


def compare_owner(n, row, words, table, tails, pay):
    sub = lax.broadcasted_iota(jnp.int32, (8, LANES), 0)
    lane = lax.broadcasted_iota(jnp.int32, (8, LANES), 1)
    choice = jnp.where(lane < 96, lane // MAIN, (lane - 96) // FRAMES)

    def pick(parts):
        return jnp.where(choice == 0, parts[0], jnp.where(choice == 1, parts[1], parts[2]))

    def operand(main, ends):
        end = jnp.concatenate([jnp.where(sub < 4, ends[0], pltpu.roll(ends[1], 4, 0)), ends[2]], axis=0)
        return main + [end.astype(jnp.bfloat16)]

    def half(h):
        query_main, query_ends, target_main, target_ends = [], [], [], []
        for t in range(3):
            slot = jnp.minimum(t * HALVES + h, SLOTS - 1)
            query = words[n, 0, slot]
            query_main.append(table[(row * COLS + n) * TILES + query])
            query_ends.append(tails[(row * COLS + n) * CLIPS + query])
            target_main.append(table[words[n, 1, slot]])
            target_ends.append(tails[words[n, 2, slot]])
        right = operand(target_main, target_ends) + [jnp.zeros((16, LANES), jnp.bfloat16)]
        product = lax.dot_general(
            jnp.concatenate(operand(query_main, query_ends), axis=0),
            jnp.concatenate(right, axis=0),
            (((1,), (1,)), ((), ())),
            preferred_element_type=jnp.float32,
        )
        main = [
            pick([product[t * MAIN + k * 8 : t * MAIN + k * 8 + 8] for t in range(3)])
            for k in range(4)
        ]
        front = product[96:104]
        end = pick([front, pltpu.roll(front, 4, 0), product[104:112]])
        return jnp.concatenate(main, axis=0).astype(jnp.bfloat16), end

    def group(g, carry):
        base = pl.multiple_of(g * GROUP_ROWS, 16)
        ends = []
        for b in range(2):
            main, end = half(g * 2 + b)
            pay[n, pl.ds(base + b * MAIN, MAIN), :] = main
            ends.append(end)
        pay[n, pl.ds(base + 2 * MAIN, 16), :] = jnp.concatenate(ends, axis=0).astype(jnp.bfloat16)
        return carry

    lax.fori_loop(0, GROUPS, group, 0)


def chamfer(got, frames):
    lane = lax.broadcasted_iota(jnp.int32, (8, LANES), 1)
    frames[...] = jnp.zeros_like(frames)

    def best(x):
        top = jnp.maximum(x, shift(x, 4))
        top = jnp.maximum(top, shift(top, 8))
        top = jnp.maximum(top, shift(top, 16))
        ends = [shift(x, 96 + t * FRAMES - 32 * t) for t in range(3)]
        end = jnp.where(lane < 32, ends[0], jnp.where(lane < 64, ends[1], ends[2]))
        return jnp.maximum(top, end)

    def group(g, carry):
        base = pl.multiple_of(g * GROUP_ROWS, 16)
        total = got[0, pl.ds(base, GROUP_ROWS), :].astype(jnp.float32)
        for m in range(1, SLICES):
            total += got[m, pl.ds(base, GROUP_ROWS), :].astype(jnp.float32)
        for b in range(2):
            main = [best(total[b * MAIN + k * 8 : b * MAIN + k * 8 + 8]) for k in range(4)]
            main = (main[0] + main[1]) + (main[2] + main[3])
            end = best(total[2 * MAIN + b * 8 : 2 * MAIN + b * 8 + 8])
            value = (main + pltpu.roll(main, 4, 0) + end) * (1.0 / REGIONS)
            for f in range(FRAMES):
                frames[f, pl.ds(g * 2 + b, 1), :] = value[f : f + 1]
        return carry

    lax.fori_loop(0, GROUPS, group, 0)


def convolve(padded, kernels):
    channels = padded.shape[3]
    rows = padded.shape[2]
    total = None
    for dy in range(3):
        wide = jnp.concatenate(
            [padded[dy : dy + 4, dx : dx + 4] for dx in range(3)], axis=-1
        ).reshape(16 * rows, 3 * channels)
        part = dot_split(wide, kernels[dy])
        total = part if total is None else total + part
    return total


def refine(frames, first, second, third, last, maps, scores, one, two):
    pairs = 72
    one[...] = jnp.zeros_like(one)
    two[...] = jnp.zeros_like(two)
    ch1 = first.shape[1]
    ch2 = second.shape[0]
    ch3 = third.shape[1]
    taps = first[...].astype(jnp.float32)
    spread = []
    for i in range(FRAMES):
        value = frames[i]
        for j in range(FRAMES):
            spread.append(
                jnp.concatenate(
                    [
                        jnp.broadcast_to(value[:, 32 * t + j : 32 * t + j + 1], (24, ch1))
                        for t in range(3)
                    ],
                    axis=0,
                )
            )
    for i in range(FRAMES):
        for j in range(FRAMES):
            total = jnp.zeros((pairs, ch1), jnp.float32)
            for tap, pos in around(i, j):
                total += spread[pos] * taps[tap : tap + 1, :]
            one[1 + i, 1 + j] = jnp.maximum(total, 0.0)
    seconds = second[...].astype(jnp.float32).T.astype(jnp.bfloat16)
    hidden = convolve(one, [seconds[dy * 3 * ch1 : (dy + 1) * 3 * ch1] for dy in range(3)])
    two[1:5, 1:5] = jnp.maximum(hidden, 0.0).reshape(4, 4, pairs, ch2)
    hidden = convolve(two, [third[dy * 3 * ch2 : (dy + 1) * 3 * ch2, :] for dy in range(3)])
    high, low = split(jnp.maximum(hidden, 0.0))
    lasts = last[...].astype(jnp.float32)
    lasts = jnp.concatenate(
        [lasts[:, tap * ch3 : (tap + 1) * ch3] for tap in range(9)]
        + [jnp.zeros((7, ch3), jnp.float32)],
        axis=0,
    ).astype(jnp.bfloat16)
    nt = (((1,), (1,)), ((), ()))
    response = lax.dot_general(high, lasts, nt, preferred_element_type=jnp.float32)
    response += lax.dot_general(low, lasts, nt, preferred_element_type=jnp.float32)
    response = response.reshape(16, pairs, response.shape[1])
    tap_lane = lax.broadcasted_iota(jnp.int32, (pairs, response.shape[2]), 1)
    out_lane = lax.broadcasted_iota(jnp.int32, (pairs, LANES), 1)
    result = jnp.zeros((pairs, LANES), jnp.float32)
    for i in range(FRAMES):
        for j in range(FRAMES):
            total = jnp.zeros((pairs, response.shape[2]), jnp.float32)
            for tap, pos in around(i, j):
                total += jnp.where(tap_lane == tap, response[pos], 0.0)
            value = jnp.sum(total, axis=1, keepdims=True)
            result = jnp.where(out_lane == i * 4 + j, value, result)
    result = jnp.clip(result, -1.0, 1.0)
    top = jnp.maximum(result, shift(result, 1))
    top = jnp.maximum(top, shift(top, 2))
    kept = (out_lane < 16) & (lax.rem(out_lane, 4) == 0)
    score = jnp.sum(jnp.where(kept, top, 0.0), axis=1, keepdims=True) * (1.0 / FRAMES)
    result = jnp.where(out_lane == 16, score, result)
    result = jnp.concatenate([result, jnp.zeros((LANES - pairs, LANES), jnp.float32)], axis=0).T
    for t in range(3):
        amount = min(HALVES, SLOTS - t * HALVES)
        place = slice(t * HALVES, t * HALVES + amount)
        maps[:, place] = result[:16, t * 24 : t * 24 + amount]
        scores[:, place] = result[16:17, t * 24 : t * 24 + amount]


def kernel(
    idx,
    feat,
    first,
    second,
    third,
    last,
    maps,
    scores,
    table,
    idx_all,
    words,
    units,
    scales,
    end_scales,
    tails,
    pay,
    got,
    frames,
    one,
    two,
    a_send,
    a_recv,
    i_send,
    i_recv,
    b_send,
    b_recv,
    p_send,
    p_recv,
    own_sem,
):
    row = lax.axis_index("row")
    me = lax.axis_index("col")
    z = row // 2
    core = lax.rem(row, 2)
    my_y = me // 4
    my_x = lax.rem(me, 4)
    rows_z = lambda step: lax.rem(z + step, 4) * 2 + core
    rows_mate = lambda step: lax.rem(z + step, 4) * 2 + 1 - core
    mate = z * 2 + 1 - core
    offset = lambda i: lax.rem(7 * i, COLS)
    to = lambda i: lax.rem(my_y + offset(i) // 4, 4) * 4 + lax.rem(my_x + lax.rem(offset(i), 4), 4)
    source = lambda i: (
        lax.rem(my_y + 4 - offset(i) // 4, 4) * 4 + lax.rem(my_x + 4 - lax.rem(offset(i), 4), 4)
    )
    blocks = lambda r, c: table.at[pl.ds((r * COLS + c) * TILES, TILES)]
    measure, fill = make_units(feat, scales, end_scales)

    def loop(start, stop, body):
        def step(i, carry):
            body(i)
            return carry

        lax.fori_loop(start, stop, step, 0)

    barrier = pltpu.get_barrier_semaphore()

    def greet(device_row, device_col):
        pl.semaphore_signal(
            barrier, inc=1, device_id=(device_row, device_col), device_id_type=MESH
        )

    loop(1, COLS, lambda i: greet(row, to(i)))
    for other in (rows_z(1), rows_z(2), rows_z(3), mate):
        greet(other, me)

    def plane_copy(src, dst, send, recv, i, n):
        return pltpu.make_async_remote_copy(
            src_ref=src,
            dst_ref=dst,
            send_sem=send.at[i],
            recv_sem=recv.at[i],
            device_id=(row, n),
            device_id_type=MESH,
        )

    idx_copy = lambda i: plane_copy(idx, idx_all.at[me], i_send, i_recv, i, to(i))
    slice_copy = lambda i: plane_copy(units.at[to(i)], blocks(row, me), a_send, a_recv, i, to(i))
    slice_arrival = lambda i: plane_copy(
        units.at[0], blocks(row, source(i)), a_send, a_recv, i, to(i)
    )
    part_copy = lambda i: plane_copy(pay.at[to(i)], got.at[me], p_send, p_recv, i, to(i))
    part_arrival = lambda i: plane_copy(pay.at[0], got.at[source(i)], p_send, p_recv, i, to(i))

    def forward(source_row, s, target_row, kind, i):
        return pltpu.make_async_remote_copy(
            src_ref=blocks(source_row, s),
            dst_ref=blocks(source_row, s),
            send_sem=b_send.at[kind, i],
            recv_sem=b_recv.at[kind, i],
            device_id=(target_row, me),
            device_id_type=MESH,
        )

    def spread(i):
        s = source(i)
        for step in (1, 3, 2):
            forward(row, s, rows_z(step), step, i).start()
        forward(row, s, mate, 4, i).start()

    measure()
    pl.semaphore_wait(barrier, COLS - 1 + 4)

    @pl.when(me < SLICES)
    def _():
        fill(blocks(row, me), me)
        spread(0)

    idx_all[me] = idx[...]
    loop(1, COLS, lambda i: idx_copy(i).start())

    def send_slice(i):
        n = to(i)

        @pl.when(n < SLICES)
        def _():
            fill(units.at[n], n)
            slice_copy(i).start()

    loop(1, COLS, send_slice)

    @pl.when(me < SLICES)
    def _():
        def pass_on(i):
            slice_arrival(i).wait_recv()
            spread(i)

        loop(1, COLS, pass_on)

        def relay(i):
            s = source(i)
            for step in (1, 3, 2):
                block_row = rows_z(4 - step)
                forward(block_row, s, rows_z(step), step, i).wait_recv()
                forward(block_row, s, mate, 4 + step, i).start()

        loop(0, COLS, relay)

        def settle(i):
            s = source(i)
            forward(rows_mate(0), s, mate, 4, i).wait_recv()
            for step in (1, 3, 2):
                forward(rows_mate(4 - step), s, mate, 4 + step, i).wait_recv()

        loop(0, COLS, settle)

    loop(1, COLS, lambda i: idx_copy(i).wait())

    @pl.when(me < SLICES)
    def _():
        local = pltpu.make_async_copy(idx_all, words, own_sem.at[0])
        local.start()

        def widen(i):
            for k in range(2):
                ends = table[i * TILES + CLIPS + k].astype(jnp.float32)
                for p in range(4):
                    pair = ends[p * 8 : p * 8 + 8]
                    tails[i * CLIPS + k * 8 + p * 2] = pair
                    tails[i * CLIPS + k * 8 + p * 2 + 1] = pltpu.roll(pair, 4, 0)

        loop(0, ROWS * COLS, widen)
        local.wait()

        def send_part(i):
            compare_owner(to(i), row, words, table, tails, pay)
            part_copy(i).start()

        loop(1, COLS, send_part)
        compare_owner(me, row, words, table, tails, pay)
        mine = pltpu.make_async_copy(pay.at[me], got.at[me], own_sem.at[1])
        mine.start()
        mine.wait()

    def take_part(i):
        @pl.when(source(i) < SLICES)
        def _():
            part_arrival(i).wait_recv()

    loop(1, COLS, take_part)
    chamfer(got, frames)
    refine(frames, first, second, third, last, maps, scores, one, two)

    def drain_slice(i):
        @pl.when(to(i) < SLICES)
        def _():
            slice_copy(i).wait_send()

    loop(1, COLS, drain_slice)

    @pl.when(me < SLICES)
    def _():
        loop(1, COLS, lambda i: part_copy(i).wait_send())

        def drain(i):
            s = source(i)
            forward(row, s, mate, 4, i).wait_send()
            for step in (1, 3, 2):
                forward(row, s, rows_z(step), step, i).wait_send()
                forward(rows_z(4 - step), s, mate, 4 + step, i).wait_send()

        loop(0, COLS, drain)


def per_device(
    features,
    query_row,
    target_device,
    target_row,
    pair_count,
    conv_first,
    conv_second,
    conv_third,
    conv_last,
):
    device = target_device[:, 0]
    asked = jnp.stack([query_row, device * TILES + target_row, device * CLIPS + target_row])
    asked = jnp.pad(asked, ((0, 5), (0, LANES - SLOTS)))
    vmem = pl.BlockSpec(memory_space=pltpu.VMEM)
    dma = pltpu.SemaphoreType.DMA
    bf16, f32, i32 = jnp.bfloat16, jnp.float32, jnp.int32
    maps, scores = pl.pallas_call(
        kernel,
        out_shape=(
            jax.ShapeDtypeStruct((FRAMES * FRAMES, SLOTS), f32),
            jax.ShapeDtypeStruct((1, SLOTS), f32),
        ),
        in_specs=[vmem] * 6,
        out_specs=[vmem] * 2,
        scratch_shapes=[
            pltpu.VMEM((ROWS * COLS * TILES, MAIN, LANES), bf16),
            pltpu.VMEM((COLS, 8, LANES), i32),
            pltpu.SMEM((COLS, 8, LANES), i32),
            pltpu.VMEM((SLICES, TILES, MAIN, LANES), bf16),
            pltpu.VMEM((CLIPS, MAIN, LANES), f32),
            pltpu.VMEM((CLIPS // 4, 16, LANES), f32),
            pltpu.VMEM((ROWS * COLS * CLIPS, 8, LANES), f32),
            pltpu.VMEM((COLS, PAY, LANES), bf16),
            pltpu.VMEM((COLS, PAY, LANES), bf16),
            pltpu.VMEM((FRAMES, 24, LANES), f32),
            pltpu.VMEM((6, 6, 72, conv_first.shape[1]), f32),
            pltpu.VMEM((6, 6, 72, conv_second.shape[1]), f32),
            dma((COLS,)),
            dma((COLS,)),
            dma((COLS,)),
            dma((COLS,)),
            dma((8, COLS)),
            dma((8, COLS)),
            dma((COLS,)),
            dma((COLS,)),
            dma((2,)),
        ],
        compiler_params=pltpu.CompilerParams(
            collective_id=0, has_side_effects=True, vmem_limit_bytes=VMEM_LIMIT
        ),
    )(
        asked,
        features.transpose(0, 2, 1, 3),
        conv_first,
        conv_second.T,
        conv_third,
        conv_last.T,
    )
    live = lax.broadcasted_iota(jnp.int32, (1, SLOTS), 1) < pair_count[0]
    return jnp.where(live, maps, 0.0).T, jnp.where(live, scores, 0.0)[0]


def solution(mesh):
    return jax.shard_map(
        per_device,
        mesh=mesh,
        in_specs=(
            P(("row", "col"), None, None, None),
            P(("row", "col")),
            P(("row", "col"), None),
            P(("row", "col")),
            P(("row", "col")),
            P(),
            P(),
            P(),
            P(),
        ),
        out_specs=(P(("row", "col"), None), P(("row", "col"))),
        check_vma=False,
    )
```

```python
import functools

import jax
import jax.numpy as jnp
from jax import lax
from jax.experimental import pallas as pl
from jax.experimental.pallas import tpu as pltpu
from jax.sharding import PartitionSpec as P

MESH = pl.DeviceIdType.MESH
CLIPS = 16
FRAMES = 4
REGIONS = 9
DIM = 1920
LANES = 128
SLICES = DIM // LANES
COLS = 16
ROWS = 8
MAIN = 32
TILES = CLIPS + CLIPS * FRAMES // MAIN
SLOTS = 64
HALVES = 22
GROUPS = HALVES // 2
ENDS = HALVES * MAIN
PAY = ENDS + 96
VMEM_LIMIT = 60 * 2**20


def split(x):
    high = x.astype(jnp.bfloat16)
    return high, (x - high.astype(jnp.float32)).astype(jnp.bfloat16)


def dot_split(x, kernel):
    high, low = split(x)
    return jnp.dot(high, kernel, preferred_element_type=jnp.float32) + jnp.dot(
        low, kernel, preferred_element_type=jnp.float32
    )


def around(i, j):
    return [
        (dy * 3 + dx, (i + dy - 1) * 4 + j + dx - 1)
        for dy in range(3)
        for dx in range(3)
        if 0 <= i + dy - 1 < 4 and 0 <= j + dx - 1 < 4
    ]


def shift(x, by):
    return pltpu.roll(x, (LANES - by) % LANES, 1)


def make_units(feat, scales, end_scales):
    def measure():
        def quad(j, carry):
            ends = []
            for k in range(4):
                c = j * 4 + k
                parts = []
                for r in range(REGIONS):
                    x = feat[c, r]
                    total = jnp.sum(x * x, axis=-1, keepdims=True)
                    parts.append(jnp.broadcast_to(1.0 / jnp.sqrt(total + 1e-06), (FRAMES, LANES)))
                scales[c] = jnp.concatenate(parts[:8], axis=0)
                ends.append(parts[8])
            end_scales[j] = jnp.concatenate(ends, axis=0)
            return carry

        lax.fori_loop(0, CLIPS // 4, quad, 0)

    def fill(block, n):
        lanes = pl.ds(pl.multiple_of(n * LANES, LANES), LANES)

        def quad(j, carry):
            ends = []
            for k in range(4):
                c = j * 4 + k
                parts = [feat[c, r, :, lanes] for r in range(REGIONS)]
                main = jnp.concatenate(parts[:8], axis=0) * scales[c]
                block[c] = main.astype(jnp.bfloat16)
                ends.append(parts[8])
            end = jnp.concatenate(ends, axis=0) * end_scales[j]
            place = pl.ds(pl.multiple_of(lax.rem(j, 2) * 16, 16), 16)
            block[CLIPS + j // 2, place, :] = end.astype(jnp.bfloat16)
            return carry

        lax.fori_loop(0, CLIPS // 4, quad, 0)

    return measure, fill


def compare_owner(n, row, words, table, tails, pay):
    sub = lax.broadcasted_iota(jnp.int32, (8, LANES), 0)
    lane = lax.broadcasted_iota(jnp.int32, (8, LANES), 1)
    choice = jnp.where(lane < 96, lane // MAIN, (lane - 96) // FRAMES)

    def pick(parts):
        return jnp.where(choice == 0, parts[0], jnp.where(choice == 1, parts[1], parts[2]))

    def operand(main, ends):
        end = jnp.concatenate([jnp.where(sub < 4, ends[0], pltpu.roll(ends[1], 4, 0)), ends[2]], axis=0)
        return main + [end.astype(jnp.bfloat16)]

    def half(h):
        query_main, query_ends, target_main, target_ends = [], [], [], []
        for t in range(3):
            slot = jnp.minimum(t * HALVES + h, SLOTS - 1)
            query = words[n, 0, slot]
            query_main.append(table[(row * COLS + n) * TILES + query])
            query_ends.append(tails[(row * COLS + n) * CLIPS + query])
            target_main.append(table[words[n, 1, slot]])
            target_ends.append(tails[words[n, 2, slot]])
        right = operand(target_main, target_ends) + [jnp.zeros((16, LANES), jnp.bfloat16)]
        product = lax.dot_general(
            jnp.concatenate(operand(query_main, query_ends), axis=0),
            jnp.concatenate(right, axis=0),
            (((1,), (1,)), ((), ())),
            preferred_element_type=jnp.float32,
        )
        main = [
            pick([product[t * MAIN + k * 8 : t * MAIN + k * 8 + 8] for t in range(3)])
            for k in range(4)
        ]
        front = product[96:104]
        end = pick([front, pltpu.roll(front, 4, 0), product[104:112]])
        return jnp.concatenate(main, axis=0).astype(jnp.bfloat16), end

    sub_low = sub < 4
    rows = []
    for g in range(GROUPS):
        ends = []
        for b in range(2):
            h = g * 2 + b
            pay[n, h * MAIN : (h + 1) * MAIN, :], end = half(h)
            ends.append(end)
        rows.append(jnp.where(sub_low, ends[0], pltpu.roll(ends[1], 4, 0)))
    rows.append(rows[-1])
    for k in range(len(rows) // 2):
        pair = jnp.concatenate(rows[2 * k : 2 * k + 2], axis=0)
        pay[n, ENDS + k * 16 : ENDS + k * 16 + 16, :] = pair.astype(jnp.bfloat16)


def chamfer(got, frames):
    lane = lax.broadcasted_iota(jnp.int32, (8, LANES), 1)
    frames[...] = jnp.zeros_like(frames)

    def best(x):
        top = jnp.maximum(x, shift(x, 4))
        top = jnp.maximum(top, shift(top, 8))
        top = jnp.maximum(top, shift(top, 16))
        ends = [shift(x, 96 + t * FRAMES - 32 * t) for t in range(3)]
        end = jnp.where(lane < 32, ends[0], jnp.where(lane < 64, ends[1], ends[2]))
        return jnp.maximum(top, end)

    def add(start, amount):
        total = got[0, pl.ds(start, amount), :].astype(jnp.float32)
        for m in range(1, SLICES):
            total += got[m, pl.ds(start, amount), :].astype(jnp.float32)
        return total

    def quad(g, carry):
        base = pl.multiple_of(g * 4 * MAIN, MAIN)
        ends = add(pl.multiple_of(ENDS + g * 16, 16), 16)
        for b in range(4):
            total = add(pl.multiple_of(base + b * MAIN, MAIN), MAIN)
            main = [best(total[k * 8 : k * 8 + 8]) for k in range(4)]
            main = (main[0] + main[1]) + (main[2] + main[3])
            main = main + pltpu.roll(main, 4, 0)
            end = best(ends[b // 2 * 8 : b // 2 * 8 + 8])
            if b % 2:
                end = pltpu.roll(end, 4, 0)
            value = (main + end) * (1.0 / REGIONS)
            for f in range(FRAMES):
                frames[f, pl.ds(g * 4 + b, 1), :] = value[f : f + 1]
        return carry

    lax.fori_loop(0, 24 // 4, quad, 0)


def convolve(padded, kernels):
    channels = padded.shape[3]
    rows = padded.shape[2]
    total = None
    for dy in range(3):
        wide = jnp.concatenate(
            [padded[dy : dy + 4, dx : dx + 4] for dx in range(3)], axis=-1
        ).reshape(16 * rows, 3 * channels)
        part = dot_split(wide, kernels[dy])
        total = part if total is None else total + part
    return total


def refine(frames, first, second, third, last, maps, scores, one, two):
    pairs = 72
    one[...] = jnp.zeros_like(one)
    two[...] = jnp.zeros_like(two)
    ch1 = first.shape[1]
    ch2 = second.shape[0]
    ch3 = third.shape[1]
    taps = first[...].astype(jnp.float32)
    spread = []
    for i in range(FRAMES):
        value = frames[i]
        for j in range(FRAMES):
            spread.append(
                jnp.concatenate(
                    [
                        jnp.broadcast_to(value[:, 32 * t + j : 32 * t + j + 1], (24, ch1))
                        for t in range(3)
                    ],
                    axis=0,
                )
            )
    for i in range(FRAMES):
        for j in range(FRAMES):
            total = jnp.zeros((pairs, ch1), jnp.float32)
            for tap, pos in around(i, j):
                total += spread[pos] * taps[tap : tap + 1, :]
            one[1 + i, 1 + j] = jnp.maximum(total, 0.0)
    seconds = second[...].astype(jnp.float32).T.astype(jnp.bfloat16)
    hidden = convolve(one, [seconds[dy * 3 * ch1 : (dy + 1) * 3 * ch1] for dy in range(3)])
    two[1:5, 1:5] = jnp.maximum(hidden, 0.0).reshape(4, 4, pairs, ch2)
    hidden = convolve(two, [third[dy * 3 * ch2 : (dy + 1) * 3 * ch2, :] for dy in range(3)])
    high, low = split(jnp.maximum(hidden, 0.0))
    lasts = last[...].astype(jnp.float32)
    lasts = jnp.concatenate(
        [lasts[:, tap * ch3 : (tap + 1) * ch3] for tap in range(9)]
        + [jnp.zeros((7, ch3), jnp.float32)],
        axis=0,
    ).astype(jnp.bfloat16)
    nt = (((1,), (1,)), ((), ()))
    response = lax.dot_general(high, lasts, nt, preferred_element_type=jnp.float32)
    response += lax.dot_general(low, lasts, nt, preferred_element_type=jnp.float32)
    response = response.reshape(16, pairs, response.shape[1])
    tap_lane = lax.broadcasted_iota(jnp.int32, (pairs, response.shape[2]), 1)
    out_lane = lax.broadcasted_iota(jnp.int32, (pairs, LANES), 1)
    result = jnp.zeros((pairs, LANES), jnp.float32)
    for i in range(FRAMES):
        for j in range(FRAMES):
            total = jnp.zeros((pairs, response.shape[2]), jnp.float32)
            for tap, pos in around(i, j):
                total += jnp.where(tap_lane == tap, response[pos], 0.0)
            value = jnp.sum(total, axis=1, keepdims=True)
            result = jnp.where(out_lane == i * 4 + j, value, result)
    result = jnp.clip(result, -1.0, 1.0)
    top = jnp.maximum(result, shift(result, 1))
    top = jnp.maximum(top, shift(top, 2))
    kept = (out_lane < 16) & (lax.rem(out_lane, 4) == 0)
    score = jnp.sum(jnp.where(kept, top, 0.0), axis=1, keepdims=True) * (1.0 / FRAMES)
    result = jnp.where(out_lane == 16, score, result)
    result = jnp.concatenate([result, jnp.zeros((LANES - pairs, LANES), jnp.float32)], axis=0).T
    for t in range(3):
        amount = min(HALVES, SLOTS - t * HALVES)
        place = slice(t * HALVES, t * HALVES + amount)
        maps[:, place] = result[:16, t * 24 : t * 24 + amount]
        scores[:, place] = result[16:17, t * 24 : t * 24 + amount]


def kernel(
    query_row,
    target_device,
    target_row,
    feat,
    first,
    second,
    third,
    last,
    maps,
    scores,
    table,
    idx,
    idx_all,
    words,
    units,
    scales,
    end_scales,
    tails,
    pay,
    got,
    frames,
    one,
    two,
    a_send,
    a_recv,
    i_send,
    i_recv,
    b_send,
    b_recv,
    p_send,
    p_recv,
    own_sem,
):
    row = lax.axis_index("row")
    me = lax.axis_index("col")
    z = row // 2
    core = lax.rem(row, 2)
    my_y = me // 4
    my_x = lax.rem(me, 4)
    rows_z = lambda step: lax.rem(z + step, 4) * 2 + core
    rows_mate = lambda step: lax.rem(z + step, 4) * 2 + 1 - core
    mate = z * 2 + 1 - core
    offset = lambda i: lax.rem(7 * i, COLS)
    to = lambda i: lax.rem(my_y + offset(i) // 4, 4) * 4 + lax.rem(my_x + lax.rem(offset(i), 4), 4)
    source = lambda i: (
        lax.rem(my_y + 4 - offset(i) // 4, 4) * 4 + lax.rem(my_x + 4 - lax.rem(offset(i), 4), 4)
    )
    blocks = lambda r, c: table.at[pl.ds((r * COLS + c) * TILES, TILES)]
    measure, fill = make_units(feat, scales, end_scales)

    def loop(start, stop, body):
        def step(i, carry):
            body(i)
            return carry

        lax.fori_loop(start, stop, step, 0)

    barrier = pltpu.get_barrier_semaphore()

    def greet(device_row, device_col):
        pl.semaphore_signal(
            barrier, inc=1, device_id=(device_row, device_col), device_id_type=MESH
        )

    loop(1, COLS, lambda i: greet(row, to(i)))
    for other in (rows_z(1), rows_z(2), rows_z(3), mate):
        greet(other, me)

    def plane_copy(src, dst, send, recv, i, n):
        return pltpu.make_async_remote_copy(
            src_ref=src,
            dst_ref=dst,
            send_sem=send.at[i],
            recv_sem=recv.at[i],
            device_id=(row, n),
            device_id_type=MESH,
        )

    idx_copy = lambda i: plane_copy(idx, idx_all.at[me], i_send, i_recv, i, to(i))
    slice_copy = lambda i: plane_copy(units.at[to(i)], blocks(row, me), a_send, a_recv, i, to(i))
    slice_arrival = lambda i: plane_copy(
        units.at[0], blocks(row, source(i)), a_send, a_recv, i, to(i)
    )
    part_copy = lambda i: plane_copy(pay.at[to(i)], got.at[me], p_send, p_recv, i, to(i))
    part_arrival = lambda i: plane_copy(pay.at[0], got.at[source(i)], p_send, p_recv, i, to(i))

    def forward(source_row, s, target_row, kind, i):
        return pltpu.make_async_remote_copy(
            src_ref=blocks(source_row, s),
            dst_ref=blocks(source_row, s),
            send_sem=b_send.at[kind, i],
            recv_sem=b_recv.at[kind, i],
            device_id=(target_row, me),
            device_id_type=MESH,
        )

    def spread(i):
        s = source(i)
        for step in (1, 3):
            forward(row, s, rows_z(step), step, i).start()
        forward(row, s, mate, 4, i).start()

    measure()
    pl.semaphore_wait(barrier, COLS - 1 + 4)

    @pl.when(me < SLICES)
    def _():
        fill(blocks(row, me), me)
        spread(0)

    idx[...] = jnp.zeros_like(idx)
    idx[0:1, :SLOTS] = query_row[...]
    idx[1:2, :SLOTS] = target_device[...] * TILES + target_row[...]
    idx[2:3, :SLOTS] = target_device[...] * CLIPS + target_row[...]
    idx_all[me] = idx[...]
    loop(1, COLS, lambda i: idx_copy(i).start())

    def send_slice(i):
        n = to(i)

        @pl.when(n < SLICES)
        def _():
            fill(units.at[n], n)
            slice_copy(i).start()

    loop(1, COLS, send_slice)

    @pl.when(me < SLICES)
    def _():
        def pass_on(i):
            slice_arrival(i).wait_recv()
            spread(i)

        loop(1, COLS, pass_on)

        def relay(i):
            s = source(i)
            for step in (1, 3):
                block_row = rows_z(4 - step)
                forward(block_row, s, rows_z(step), step, i).wait_recv()

                @pl.when(lax.rem(i, 2) == step // 2)
                def _():
                    forward(block_row, s, rows_z(step), 2, i).start()

                forward(block_row, s, mate, 4 + step, i).start()

        loop(0, COLS, relay)

        def relay_far(i):
            s = source(i)
            forward(rows_z(2), s, rows_z(1), 2, i).wait_recv()
            forward(rows_z(2), s, mate, 6, i).start()

        loop(0, COLS, relay_far)

        def settle(i):
            s = source(i)
            forward(rows_mate(0), s, mate, 4, i).wait_recv()
            for step in (1, 3, 2):
                forward(rows_mate(4 - step), s, mate, 4 + step, i).wait_recv()

        loop(0, COLS, settle)

    loop(1, COLS, lambda i: idx_copy(i).wait())

    @pl.when(me < SLICES)
    def _():
        local = pltpu.make_async_copy(idx_all, words, own_sem.at[0])
        local.start()

        def widen(i):
            for k in range(2):
                ends = table[i * TILES + CLIPS + k].astype(jnp.float32)
                for p in range(4):
                    pair = ends[p * 8 : p * 8 + 8]
                    tails[i * CLIPS + k * 8 + p * 2] = pair
                    tails[i * CLIPS + k * 8 + p * 2 + 1] = pltpu.roll(pair, 4, 0)

        loop(0, ROWS * COLS, widen)
        local.wait()

        def send_part(i):
            compare_owner(to(i), row, words, table, tails, pay)

            @pl.when(i < COLS)
            def _():
                part_copy(i).start()

        loop(1, COLS + 1, send_part)
        mine = pltpu.make_async_copy(pay.at[me], got.at[me], own_sem.at[1])
        mine.start()
        mine.wait()

    def take_part(i):
        @pl.when(source(i) < SLICES)
        def _():
            part_arrival(i).wait_recv()

    loop(1, COLS, take_part)
    chamfer(got, frames)
    refine(frames, first, second, third, last, maps, scores, one, two)

    def drain_slice(i):
        @pl.when(to(i) < SLICES)
        def _():
            slice_copy(i).wait_send()

    loop(1, COLS, drain_slice)

    @pl.when(me < SLICES)
    def _():
        loop(1, COLS, lambda i: part_copy(i).wait_send())

        def drain(i):
            s = source(i)
            forward(row, s, mate, 4, i).wait_send()
            for step in (1, 3):
                block_row = rows_z(4 - step)
                forward(row, s, rows_z(step), step, i).wait_send()
                forward(block_row, s, mate, 4 + step, i).wait_send()

                @pl.when(lax.rem(i, 2) == step // 2)
                def _():
                    forward(block_row, s, rows_z(step), 2, i).wait_send()

            forward(rows_z(2), s, mate, 6, i).wait_send()

        loop(0, COLS, drain)


def per_device(
    features,
    query_row,
    target_device,
    target_row,
    pair_count,
    conv_first,
    conv_second,
    conv_third,
    conv_last,
):
    vmem = pl.BlockSpec(memory_space=pltpu.VMEM)
    dma = pltpu.SemaphoreType.DMA
    bf16, f32, i32 = jnp.bfloat16, jnp.float32, jnp.int32
    maps, scores = pl.pallas_call(
        kernel,
        out_shape=(
            jax.ShapeDtypeStruct((FRAMES * FRAMES, SLOTS), f32),
            jax.ShapeDtypeStruct((1, SLOTS), f32),
        ),
        in_specs=[vmem] * 8,
        out_specs=[vmem] * 2,
        scratch_shapes=[
            pltpu.VMEM((ROWS * COLS * TILES, MAIN, LANES), bf16),
            pltpu.VMEM((8, LANES), i32),
            pltpu.VMEM((COLS, 8, LANES), i32),
            pltpu.SMEM((COLS, 8, LANES), i32),
            pltpu.VMEM((SLICES, TILES, MAIN, LANES), bf16),
            pltpu.VMEM((CLIPS, MAIN, LANES), f32),
            pltpu.VMEM((CLIPS // 4, 16, LANES), f32),
            pltpu.VMEM((ROWS * COLS * CLIPS, 8, LANES), f32),
            pltpu.VMEM((COLS, PAY, LANES), bf16),
            pltpu.VMEM((COLS, PAY, LANES), bf16),
            pltpu.VMEM((FRAMES, 24, LANES), f32),
            pltpu.VMEM((6, 6, 72, conv_first.shape[1]), f32),
            pltpu.VMEM((6, 6, 72, conv_second.shape[1]), f32),
            dma((COLS,)),
            dma((COLS,)),
            dma((COLS,)),
            dma((COLS,)),
            dma((8, COLS)),
            dma((8, COLS)),
            dma((COLS,)),
            dma((COLS,)),
            dma((2,)),
        ],
        compiler_params=pltpu.CompilerParams(
            collective_id=0, has_side_effects=True, vmem_limit_bytes=VMEM_LIMIT
        ),
    )(
        query_row.reshape(1, SLOTS),
        target_device.reshape(1, SLOTS),
        target_row.reshape(1, SLOTS),
        features.transpose(0, 2, 1, 3),
        conv_first,
        conv_second.T,
        conv_third,
        conv_last.T,
    )
    live = lax.broadcasted_iota(jnp.int32, (1, SLOTS), 1) < pair_count[0]
    return jnp.where(live, maps, 0.0).T, jnp.where(live, scores, 0.0)[0]


def solution(mesh):
    return jax.shard_map(
        per_device,
        mesh=mesh,
        in_specs=(
            P(("row", "col"), None, None, None),
            P(("row", "col")),
            P(("row", "col"), None),
            P(("row", "col")),
            P(("row", "col")),
            P(),
            P(),
            P(),
            P(),
        ),
        out_specs=(P(("row", "col"), None), P(("row", "col"))),
        check_vma=False,
    )
```

```python
import functools

import jax
import jax.numpy as jnp
from jax import lax
from jax.experimental import pallas as pl
from jax.experimental.pallas import tpu as pltpu
from jax.sharding import PartitionSpec as P

MESH = pl.DeviceIdType.MESH
CLIPS = 16
FRAMES = 4
REGIONS = 9
DIM = 1920
LANES = 128
SLICES = DIM // LANES
COLS = 16
ROWS = 8
MAIN = 32
TILES = CLIPS + CLIPS * FRAMES // MAIN
SLOTS = 64
HALVES = 22
PAIRS = 72
QUAD = 4 * MAIN + 16
STAGES = ((0, 0, 8), (4, 8, 4), (8, 12, 4), (14, 16, 4), (16, 20, 2))
STARTS = tuple(first // 4 * QUAD for _, first, _ in STAGES)
SIZES = tuple(amount * MAIN + -(-amount // 4) * 16 for _, _, amount in STAGES)
PAY = STARTS[-1] + SIZES[-1]
VMEM_LIMIT = 60 * 2**20


def split(x):
    high = x.astype(jnp.bfloat16)
    return high, (x - high.astype(jnp.float32)).astype(jnp.bfloat16)


def dot_split(x, kernel):
    high, low = split(x)
    return jnp.dot(high, kernel, preferred_element_type=jnp.float32) + jnp.dot(
        low, kernel, preferred_element_type=jnp.float32
    )


def around(i, j):
    return [
        (dy * 3 + dx, (i + dy - 1) * 4 + j + dx - 1)
        for dy in range(3)
        for dx in range(3)
        if 0 <= i + dy - 1 < 4 and 0 <= j + dx - 1 < 4
    ]


def shift(x, by):
    return pltpu.roll(x, (LANES - by) % LANES, 1)


def make_units(feat, scales, end_scales):
    def measure():
        def quad(j, carry):
            ends = []
            for k in range(4):
                c = j * 4 + k
                parts = []
                for r in range(REGIONS):
                    x = feat[c, r]
                    total = jnp.sum(x * x, axis=-1, keepdims=True)
                    parts.append(jnp.broadcast_to(1.0 / jnp.sqrt(total + 1e-06), (FRAMES, LANES)))
                scales[c] = jnp.concatenate(parts[:8], axis=0)
                ends.append(parts[8])
            end_scales[j] = jnp.concatenate(ends, axis=0)
            return carry

        lax.fori_loop(0, CLIPS // 4, quad, 0)

    def fill(block, n):
        lanes = pl.ds(pl.multiple_of(n * LANES, LANES), LANES)

        def quad(j, carry):
            ends = []
            for k in range(4):
                c = j * 4 + k
                parts = [feat[c, r, :, lanes] for r in range(REGIONS)]
                main = jnp.concatenate(parts[:8], axis=0) * scales[c]
                block[c] = main.astype(jnp.bfloat16)
                ends.append(parts[8])
            end = jnp.concatenate(ends, axis=0) * end_scales[j]
            place = pl.ds(pl.multiple_of(lax.rem(j, 2) * 16, 16), 16)
            block[CLIPS + j // 2, place, :] = end.astype(jnp.bfloat16)
            return carry

        lax.fori_loop(0, CLIPS // 4, quad, 0)

    return measure, fill


def sort_kernel(count, query_row, target_device, target_row, idx, place):
    z = lax.axis_index("row") // 2
    a = lax.broadcasted_iota(jnp.int32, (LANES, LANES), 0)
    b = lax.broadcasted_iota(jnp.int32, (LANES, LANES), 1)

    def lines(x):
        wide = jnp.concatenate([x, jnp.zeros((1, LANES - SLOTS), jnp.int32)], axis=1)
        wide = jnp.broadcast_to(wide.astype(jnp.float32), (LANES, LANES))
        return wide, wide.T

    device = target_device[...]
    far = (device >> 5) == lax.rem(z + 2, 4)
    key_b, key_a = lines(jnp.where(far, 1 + (device & 15), 0))
    earlier = (a < SLOTS) & ((key_a < key_b) | ((key_a == key_b) & (a < b)))
    rank_b = jnp.sum(earlier.astype(jnp.float32), axis=0, keepdims=True)
    earlier = (b < SLOTS) & ((key_b < key_a) | ((key_b == key_a) & (b < a)))
    rank_a = jnp.sum(earlier.astype(jnp.float32), axis=1, keepdims=True)
    taken = (rank_a == b.astype(jnp.float32)) & (a < SLOTS)

    def ordered(x):
        kept = jnp.where(taken, lines(x)[1], 0.0)
        return jnp.sum(kept, axis=0, keepdims=True).astype(jnp.int32)

    rows = [ordered(query_row[...]), ordered(device * CLIPS + target_row[...])]
    idx[...] = jnp.concatenate(rows + [jnp.zeros((6, LANES), jnp.int32)], axis=0)
    position = (3 * lax.rem(a, 24) + a // 24).astype(jnp.float32)
    match = (position == rank_b) & (a < PAIRS) & (b < SLOTS) & (b < count[0])
    place[...] = jnp.where(match, 1.0, 0.0).astype(jnp.bfloat16)


def sort_slots(count, query_row, target_device, target_row):
    vmem = pl.BlockSpec(memory_space=pltpu.VMEM)
    return pl.pallas_call(
        sort_kernel,
        out_shape=(
            jax.ShapeDtypeStruct((8, LANES), jnp.int32),
            jax.ShapeDtypeStruct((LANES, LANES), jnp.bfloat16),
        ),
        in_specs=[pl.BlockSpec(memory_space=pltpu.SMEM)] + [vmem] * 3,
        out_specs=[vmem] * 2,
    )(count, query_row, target_device, target_row)


def compare_owner(n, stage, row, words, mains, tails, pay):
    sub = lax.broadcasted_iota(jnp.int32, (8, LANES), 0)
    lane = lax.broadcasted_iota(jnp.int32, (8, LANES), 1)
    choice = jnp.where(lane < 96, lane // MAIN, (lane - 96) // FRAMES)

    def pick(parts):
        return jnp.where(choice == 0, parts[0], jnp.where(choice == 1, parts[1], parts[2]))

    def operand(main, ends):
        end = jnp.concatenate([jnp.where(sub < 4, ends[0], pltpu.roll(ends[1], 4, 0)), ends[2]], axis=0)
        return main + [end.astype(jnp.bfloat16)]

    def half(h):
        query_main, query_ends, target_main, target_ends = [], [], [], []
        for t in range(3):
            slot = min(3 * h + t, SLOTS - 1)
            query = words[n, 0, slot]
            target = words[n, 1, slot]
            query_main.append(mains[(row * COLS + n) * CLIPS + query])
            query_ends.append(tails[(row * COLS + n) * CLIPS + query])
            target_main.append(mains[target])
            target_ends.append(tails[target])
        right = operand(target_main, target_ends) + [jnp.zeros((16, LANES), jnp.bfloat16)]
        product = lax.dot_general(
            jnp.concatenate(operand(query_main, query_ends), axis=0),
            jnp.concatenate(right, axis=0),
            (((1,), (1,)), ((), ())),
            preferred_element_type=jnp.float32,
        )
        main = [
            pick([product[t * MAIN + k * 8 : t * MAIN + k * 8 + 8] for t in range(3)])
            for k in range(4)
        ]
        front = product[96:104]
        end = pick([front, pltpu.roll(front, 4, 0), product[104:112]])
        return jnp.concatenate(main, axis=0).astype(jnp.bfloat16), end

    _, first, amount = STAGES[stage]
    for base in range(0, amount, 4):
        start = STARTS[stage] + base // 4 * QUAD
        several = min(4, amount - base)
        rows = []
        for b in range(0, several, 2):
            ends = []
            for k in (b, b + 1):
                pay[n, start + k * MAIN : start + (k + 1) * MAIN, :], end = half(first + base + k)
                ends.append(end)
            rows.append(jnp.where(sub < 4, ends[0], pltpu.roll(ends[1], 4, 0)))
        rows = jnp.concatenate([rows[0], rows[-1]], axis=0).astype(jnp.bfloat16)
        pay[n, start + several * MAIN : start + several * MAIN + 16, :] = rows


def chamfer(got, frames, first, stop):
    lane = lax.broadcasted_iota(jnp.int32, (8, LANES), 1)

    def best(x):
        top = jnp.maximum(x, shift(x, 4))
        top = jnp.maximum(top, shift(top, 8))
        top = jnp.maximum(top, shift(top, 16))
        ends = [shift(x, 96 + t * FRAMES - 32 * t) for t in range(3)]
        end = jnp.where(lane < 32, ends[0], jnp.where(lane < 64, ends[1], ends[2]))
        return jnp.maximum(top, end)

    def add(start, amount):
        total = got[0, pl.ds(start, amount), :].astype(jnp.float32)
        for m in range(1, SLICES):
            total += got[m, pl.ds(start, amount), :].astype(jnp.float32)
        return total

    def quad(q, amount):
        base = pl.multiple_of(q * QUAD, 16)
        ends = add(pl.multiple_of(base + amount * MAIN, 16), 16)
        for b in range(amount):
            total = add(pl.multiple_of(base + b * MAIN, 16), MAIN)
            main = [best(total[k * 8 : k * 8 + 8]) for k in range(4)]
            main = (main[0] + main[1]) + (main[2] + main[3])
            main = main + pltpu.roll(main, 4, 0)
            end = best(ends[b // 2 * 8 : b // 2 * 8 + 8])
            if b % 2:
                end = pltpu.roll(end, 4, 0)
            value = (main + end) * (1.0 / REGIONS)
            for f in range(FRAMES):
                frames[f, pl.ds(q * 4 + b, 1), :] = value[f : f + 1]

    if (stop - first) % 4:
        quad(first // 4, stop - first)
    else:

        def step(q, carry):
            quad(q, 4)
            return carry

        lax.fori_loop(first // 4, stop // 4, step, 0)


def convolve(padded, kernels):
    channels = padded.shape[3]
    rows = padded.shape[2]
    total = None
    for dy in range(3):
        wide = jnp.concatenate(
            [padded[dy : dy + 4, dx : dx + 4] for dx in range(3)], axis=-1
        ).reshape(16 * rows, 3 * channels)
        part = dot_split(wide, kernels[dy])
        total = part if total is None else total + part
    return total


def refine(frames, place, first, second, third, last, maps, scores, one, two):
    pairs = PAIRS
    one[...] = jnp.zeros_like(one)
    two[...] = jnp.zeros_like(two)
    ch1 = first.shape[1]
    ch2 = second.shape[0]
    ch3 = third.shape[1]
    taps = first[...].astype(jnp.float32)
    spread = []
    for i in range(FRAMES):
        value = frames[i]
        for j in range(FRAMES):
            spread.append(
                jnp.concatenate(
                    [
                        jnp.broadcast_to(value[:, 32 * t + j : 32 * t + j + 1], (24, ch1))
                        for t in range(3)
                    ],
                    axis=0,
                )
            )
    for i in range(FRAMES):
        for j in range(FRAMES):
            total = jnp.zeros((pairs, ch1), jnp.float32)
            for tap, pos in around(i, j):
                total += spread[pos] * taps[tap : tap + 1, :]
            one[1 + i, 1 + j] = jnp.maximum(total, 0.0)
    seconds = second[...].astype(jnp.float32).T.astype(jnp.bfloat16)
    hidden = convolve(one, [seconds[dy * 3 * ch1 : (dy + 1) * 3 * ch1] for dy in range(3)])
    two[1:5, 1:5] = jnp.maximum(hidden, 0.0).reshape(4, 4, pairs, ch2)
    hidden = convolve(two, [third[dy * 3 * ch2 : (dy + 1) * 3 * ch2, :] for dy in range(3)])
    high, low = split(jnp.maximum(hidden, 0.0))
    lasts = last[...].astype(jnp.float32)
    lasts = jnp.concatenate(
        [lasts[:, tap * ch3 : (tap + 1) * ch3] for tap in range(9)]
        + [jnp.zeros((7, ch3), jnp.float32)],
        axis=0,
    ).astype(jnp.bfloat16)
    nt = (((1,), (1,)), ((), ()))
    response = lax.dot_general(high, lasts, nt, preferred_element_type=jnp.float32)
    response += lax.dot_general(low, lasts, nt, preferred_element_type=jnp.float32)
    response = response.reshape(16, pairs, response.shape[1])
    tap_lane = lax.broadcasted_iota(jnp.int32, (pairs, response.shape[2]), 1)
    out_lane = lax.broadcasted_iota(jnp.int32, (pairs, LANES), 1)
    result = jnp.zeros((pairs, LANES), jnp.float32)
    for i in range(FRAMES):
        for j in range(FRAMES):
            total = jnp.zeros((pairs, response.shape[2]), jnp.float32)
            for tap, pos in around(i, j):
                total += jnp.where(tap_lane == tap, response[pos], 0.0)
            value = jnp.sum(total, axis=1, keepdims=True)
            result = jnp.where(out_lane == i * 4 + j, value, result)
    result = jnp.clip(result, -1.0, 1.0)
    top = jnp.maximum(result, shift(result, 1))
    top = jnp.maximum(top, shift(top, 2))
    kept = (out_lane < 16) & (lax.rem(out_lane, 4) == 0)
    score = jnp.sum(jnp.where(kept, top, 0.0), axis=1, keepdims=True) * (1.0 / FRAMES)
    result = jnp.where(out_lane == 16, score, result)
    result = jnp.concatenate([result, jnp.zeros((LANES - pairs, LANES), jnp.float32)], axis=0).T
    result = result[:24]
    high, low = split(result)
    rest = result - high.astype(jnp.float32) - low.astype(jnp.float32)
    result = sum(
        jnp.dot(part, place[...], preferred_element_type=jnp.float32)
        for part in (rest.astype(jnp.bfloat16), low, high)
    )
    maps[...] = result[:16, :SLOTS]
    scores[...] = result[16:17, :SLOTS]


def kernel(
    idx,
    place,
    feat,
    first,
    second,
    third,
    last,
    maps,
    scores,
    table,
    idx_all,
    words,
    units,
    scales,
    end_scales,
    mains,
    tails,
    pay,
    got,
    frames,
    one,
    two,
    a_send,
    a_recv,
    i_send,
    i_recv,
    b_send,
    b_recv,
    p_send,
    p_recv,
    own_sem,
):
    row = lax.axis_index("row")
    me = lax.axis_index("col")
    z = row // 2
    core = lax.rem(row, 2)
    my_y = me // 4
    my_x = lax.rem(me, 4)
    rows_z = lambda step: lax.rem(z + step, 4) * 2 + core
    rows_mate = lambda step: lax.rem(z + step, 4) * 2 + 1 - core
    mate = z * 2 + 1 - core
    offset = lambda i: lax.rem(7 * i, COLS)
    to = lambda i: lax.rem(my_y + offset(i) // 4, 4) * 4 + lax.rem(my_x + lax.rem(offset(i), 4), 4)
    source = lambda i: (
        lax.rem(my_y + 4 - offset(i) // 4, 4) * 4 + lax.rem(my_x + 4 - lax.rem(offset(i), 4), 4)
    )
    blocks = lambda r, c: table.at[pl.ds((r * COLS + c) * TILES, TILES)]
    measure, fill = make_units(feat, scales, end_scales)

    def loop(start, stop, body):
        def step(i, carry):
            body(i)
            return carry

        lax.fori_loop(start, stop, step, 0)

    barrier = pltpu.get_barrier_semaphore()

    def greet(device_row, device_col):
        pl.semaphore_signal(
            barrier, inc=1, device_id=(device_row, device_col), device_id_type=MESH
        )

    loop(1, COLS, lambda i: greet(row, to(i)))
    for other in (rows_z(1), rows_z(2), rows_z(3), mate):
        greet(other, me)

    def plane_copy(src, dst, send, recv, i, n):
        return pltpu.make_async_remote_copy(
            src_ref=src,
            dst_ref=dst,
            send_sem=send.at[i],
            recv_sem=recv.at[i],
            device_id=(row, n),
            device_id_type=MESH,
        )

    idx_copy = lambda i: plane_copy(idx, idx_all.at[me], i_send, i_recv, i, to(i))
    slice_copy = lambda i: plane_copy(units.at[to(i)], blocks(row, me), a_send, a_recv, i, to(i))
    slice_arrival = lambda i: plane_copy(
        units.at[0], blocks(row, source(i)), a_send, a_recv, i, to(i)
    )

    def part(buffer, n, stage):
        return buffer.at[n, pl.ds(STARTS[stage], SIZES[stage])]

    def part_copy(i, stage):
        return plane_copy(
            part(pay, to(i), stage),
            part(got, me, stage),
            p_send.at[stage],
            p_recv.at[stage],
            i,
            to(i),
        )

    def part_arrival(i, stage):
        return plane_copy(
            part(pay, 0, stage),
            part(got, source(i), stage),
            p_send.at[stage],
            p_recv.at[stage],
            i,
            to(i),
        )

    def own_part(stage):
        return pltpu.make_async_copy(
            part(pay, me, stage), part(got, me, stage), own_sem.at[1 + stage]
        )

    def forward(source_row, s, target_row, kind):
        return pltpu.make_async_remote_copy(
            src_ref=blocks(source_row, s),
            dst_ref=blocks(source_row, s),
            send_sem=b_send.at[kind, s],
            recv_sem=b_recv.at[kind, s],
            device_id=(target_row, me),
            device_id_type=MESH,
        )

    def spread(i):
        s = source(i)
        for step in (1, 3):
            forward(row, s, rows_z(step), step).start()
        forward(row, s, mate, 4).start()

    measure()
    pl.semaphore_wait(barrier, COLS - 1 + 4)

    @pl.when(me < SLICES)
    def _():
        fill(blocks(row, me), me)
        spread(0)

    idx_all[me] = idx[...]
    loop(1, COLS, lambda i: idx_copy(i).start())

    def send_slice(i):
        n = to(i)

        @pl.when(n < SLICES)
        def _():
            fill(units.at[n], n)
            slice_copy(i).start()

    loop(1, COLS, send_slice)

    @pl.when(me < SLICES)
    def _():
        def pass_on(i):
            slice_arrival(i).wait_recv()
            spread(i)

        loop(1, COLS, pass_on)

        def relay(s):
            for step in (1, 3):
                block_row = rows_z(4 - step)
                forward(block_row, s, rows_z(step), step).wait_recv()

                @pl.when(lax.rem(s, 2) == step // 2)
                def _():
                    forward(block_row, s, rows_z(step), 2).start()

                forward(block_row, s, mate, 4 + step).start()

        loop(0, COLS, relay)

        def settle(s):
            forward(rows_mate(0), s, mate, 4).wait_recv()
            forward(rows_mate(3), s, mate, 5).wait_recv()
            forward(rows_mate(1), s, mate, 7).wait_recv()

        loop(0, COLS, settle)

    loop(1, COLS, lambda i: idx_copy(i).wait())

    @pl.when(me < SLICES)
    def _():
        local = pltpu.make_async_copy(idx_all, words, own_sem.at[0])
        local.start()

        def settle_block(block_row, s):
            i = block_row * COLS + s
            for c in range(CLIPS):
                mains[i * CLIPS + c] = table[i * TILES + c]
            for k in range(2):
                ends = table[i * TILES + CLIPS + k].astype(jnp.float32)
                for p in range(4):
                    pair = ends[p * 8 : p * 8 + 8]
                    tails[i * CLIPS + k * 8 + p * 2] = pair
                    tails[i * CLIPS + k * 8 + p * 2 + 1] = pltpu.roll(pair, 4, 0)

        def settle_near(k):
            step = k // 32
            block_row = lax.rem(z + step + step // 2, 4) * 2 + lax.rem(k // COLS, 2)
            settle_block(block_row, lax.rem(k, COLS))

        loop(0, 6 * COLS, settle_near)
        local.wait()
        begin = 0
        for stage, (stop, _, _) in enumerate(STAGES):

            def relay_far(s):
                forward(rows_z(2), s, rows_z(1), 2).wait_recv()
                forward(rows_z(2), s, mate, 6).start()

            def settle_far(s):
                forward(rows_mate(2), s, mate, 6).wait_recv()
                settle_block(rows_z(2), s)
                settle_block(rows_mate(2), s)

            if stop > begin:
                loop(begin, stop, relay_far)
                loop(begin, stop, settle_far)
            begin = stop

            def send_part(i, stage=stage):
                compare_owner(to(i), stage, row, words, mains, tails, pay)

                @pl.when(i < COLS)
                def _():
                    part_copy(i, stage).start()

            loop(1, COLS + 1, send_part)
            own_part(stage).start()

    frames[...] = jnp.zeros_like(frames)
    for stage, (_, first_group, amount) in enumerate(STAGES):

        def take_part(i, stage=stage):
            @pl.when(source(i) < SLICES)
            def _():
                part_arrival(i, stage).wait_recv()

        loop(1, COLS, take_part)

        @pl.when(me < SLICES)
        def _(stage=stage):
            own_part(stage).wait()

        chamfer(got, frames, first_group, first_group + amount)
    refine(frames, place, first, second, third, last, maps, scores, one, two)

    def drain_slice(i):
        @pl.when(to(i) < SLICES)
        def _():
            slice_copy(i).wait_send()

    loop(1, COLS, drain_slice)

    @pl.when(me < SLICES)
    def _():
        for stage in range(len(STAGES)):
            loop(1, COLS, lambda i, stage=stage: part_copy(i, stage).wait_send())

        def drain(s):
            forward(row, s, mate, 4).wait_send()
            for step in (1, 3):
                block_row = rows_z(4 - step)
                forward(row, s, rows_z(step), step).wait_send()
                forward(block_row, s, mate, 4 + step).wait_send()

                @pl.when(lax.rem(s, 2) == step // 2)
                def _():
                    forward(block_row, s, rows_z(step), 2).wait_send()

            forward(rows_z(2), s, mate, 6).wait_send()

        loop(0, COLS, drain)


def per_device(
    features,
    query_row,
    target_device,
    target_row,
    pair_count,
    conv_first,
    conv_second,
    conv_third,
    conv_last,
):
    idx, place = sort_slots(
        pair_count,
        query_row.reshape(1, SLOTS),
        target_device.reshape(1, SLOTS),
        target_row.reshape(1, SLOTS),
    )
    vmem = pl.BlockSpec(memory_space=pltpu.VMEM)
    dma = pltpu.SemaphoreType.DMA
    bf16, f32, i32 = jnp.bfloat16, jnp.float32, jnp.int32
    maps, scores = pl.pallas_call(
        kernel,
        out_shape=(
            jax.ShapeDtypeStruct((FRAMES * FRAMES, SLOTS), f32),
            jax.ShapeDtypeStruct((1, SLOTS), f32),
        ),
        in_specs=[vmem] * 7,
        out_specs=[vmem] * 2,
        scratch_shapes=[
            pltpu.VMEM((ROWS * COLS * TILES, MAIN, LANES), bf16),
            pltpu.VMEM((COLS, 8, LANES), i32),
            pltpu.SMEM((COLS, 8, LANES), i32),
            pltpu.VMEM((SLICES, TILES, MAIN, LANES), bf16),
            pltpu.VMEM((CLIPS, MAIN, LANES), f32),
            pltpu.VMEM((CLIPS // 4, 16, LANES), f32),
            pltpu.VMEM((ROWS * COLS * CLIPS, MAIN, LANES), bf16),
            pltpu.VMEM((ROWS * COLS * CLIPS, 8, LANES), f32),
            pltpu.VMEM((COLS, PAY, LANES), bf16),
            pltpu.VMEM((COLS, PAY, LANES), bf16),
            pltpu.VMEM((FRAMES, 24, LANES), f32),
            pltpu.VMEM((6, 6, 72, conv_first.shape[1]), f32),
            pltpu.VMEM((6, 6, 72, conv_second.shape[1]), f32),
            dma((COLS,)),
            dma((COLS,)),
            dma((COLS,)),
            dma((COLS,)),
            dma((8, COLS)),
            dma((8, COLS)),
            dma((len(STAGES), COLS)),
            dma((len(STAGES), COLS)),
            dma((1 + len(STAGES),)),
        ],
        compiler_params=pltpu.CompilerParams(
            collective_id=0, has_side_effects=True, vmem_limit_bytes=VMEM_LIMIT
        ),
    )(
        idx,
        place,
        features.transpose(0, 2, 1, 3),
        conv_first,
        conv_second.T,
        conv_third,
        conv_last.T,
    )
    return maps.T, scores[0]


def solution(mesh):
    return jax.shard_map(
        per_device,
        mesh=mesh,
        in_specs=(
            P(("row", "col"), None, None, None),
            P(("row", "col")),
            P(("row", "col"), None),
            P(("row", "col")),
            P(("row", "col")),
            P(),
            P(),
            P(),
            P(),
        ),
        out_specs=(P(("row", "col"), None), P(("row", "col"))),
        check_vma=False,
    )
```

```python
import functools

import jax
import jax.numpy as jnp
from jax import lax
from jax.experimental import pallas as pl
from jax.experimental.pallas import tpu as pltpu
from jax.sharding import PartitionSpec as P

MESH = pl.DeviceIdType.MESH
CLIPS = 16
FRAMES = 4
REGIONS = 9
DIM = 1920
LANES = 128
SLICES = DIM // LANES
COLS = 16
ROWS = 8
MAIN = 32
TILES = CLIPS + CLIPS * FRAMES // MAIN
SLOTS = 64
HALVES = 22
PAIRS = 72
QUAD = 4 * MAIN + 16
STAGES = ((0, 0, 8), (4, 8, 4), (8, 12, 4), (14, 16, 4), (16, 20, 2))
STARTS = tuple(first // 4 * QUAD for _, first, _ in STAGES)
SIZES = tuple(amount * MAIN + -(-amount // 4) * 16 for _, _, amount in STAGES)
PAY = STARTS[-1] + SIZES[-1]
AHEAD = 4
VMEM_LIMIT = 62 * 2**20


def split(x):
    high = x.astype(jnp.bfloat16)
    return high, (x - high.astype(jnp.float32)).astype(jnp.bfloat16)


def dot_split(x, kernel):
    high, low = split(x)
    return jnp.dot(high, kernel, preferred_element_type=jnp.float32) + jnp.dot(
        low, kernel, preferred_element_type=jnp.float32
    )


def around(i, j):
    return [
        (dy * 3 + dx, (i + dy - 1) * 4 + j + dx - 1)
        for dy in range(3)
        for dx in range(3)
        if 0 <= i + dy - 1 < 4 and 0 <= j + dx - 1 < 4
    ]


def shift(x, by):
    return pltpu.roll(x, (LANES - by) % LANES, 1)


def make_units(load, feat, scales, end_scales):
    def measure():
        def quad(j, carry):
            ends = []
            for k in range(4):
                c = j * 4 + k
                load(c).wait()
                parts = []
                for r in range(REGIONS):
                    x = feat[c, r]
                    total = jnp.sum(x * x, axis=-1, keepdims=True)
                    parts.append(jnp.broadcast_to(1.0 / jnp.sqrt(total + 1e-06), (FRAMES, LANES)))
                scales[c] = jnp.concatenate(parts[:8], axis=0)
                ends.append(parts[8])
            end_scales[j] = jnp.concatenate(ends, axis=0)
            return carry

        lax.fori_loop(0, CLIPS // 4, quad, 0)

    def fill(block, n):
        lanes = pl.ds(pl.multiple_of(n * LANES, LANES), LANES)

        def quad(j, carry):
            ends = []
            for k in range(4):
                c = j * 4 + k
                parts = [feat[c, r, :, lanes] for r in range(REGIONS)]
                main = jnp.concatenate(parts[:8], axis=0) * scales[c]
                block[c] = main.astype(jnp.bfloat16)
                ends.append(parts[8])
            end = jnp.concatenate(ends, axis=0) * end_scales[j]
            place = pl.ds(pl.multiple_of(lax.rem(j, 2) * 16, 16), 16)
            block[CLIPS + j // 2, place, :] = end.astype(jnp.bfloat16)
            return carry

        lax.fori_loop(0, CLIPS // 4, quad, 0)

    return measure, fill


def sort_kernel(count, query_row, target_device, target_row, idx, place):
    z = lax.axis_index("row") // 2
    a = lax.broadcasted_iota(jnp.int32, (LANES, LANES), 0)
    b = lax.broadcasted_iota(jnp.int32, (LANES, LANES), 1)

    def lines(x):
        wide = jnp.concatenate([x, jnp.zeros((1, LANES - SLOTS), jnp.int32)], axis=1)
        wide = jnp.broadcast_to(wide.astype(jnp.float32), (LANES, LANES))
        return wide, wide.T

    device = target_device[...]
    far = (device >> 5) == lax.rem(z + 2, 4)
    key_b, key_a = lines(jnp.where(far, 1 + (device & 15), 0))
    earlier = (a < SLOTS) & ((key_a < key_b) | ((key_a == key_b) & (a < b)))
    rank_b = jnp.sum(earlier.astype(jnp.float32), axis=0, keepdims=True)
    earlier = (b < SLOTS) & ((key_b < key_a) | ((key_b == key_a) & (b < a)))
    rank_a = jnp.sum(earlier.astype(jnp.float32), axis=1, keepdims=True)
    taken = (rank_a == b.astype(jnp.float32)) & (a < SLOTS)

    def ordered(x):
        kept = jnp.where(taken, lines(x)[1], 0.0)
        return jnp.sum(kept, axis=0, keepdims=True).astype(jnp.int32)

    rows = [ordered(query_row[...]), ordered(device * CLIPS + target_row[...])]
    idx[...] = jnp.concatenate(rows + [jnp.zeros((6, LANES), jnp.int32)], axis=0)
    position = (3 * lax.rem(a, 24) + a // 24).astype(jnp.float32)
    match = (position == rank_b) & (a < PAIRS) & (b < SLOTS) & (b < count[0])
    place[...] = jnp.where(match, 1.0, 0.0).astype(jnp.bfloat16)


def sort_slots(count, query_row, target_device, target_row):
    vmem = pl.BlockSpec(memory_space=pltpu.VMEM)
    return pl.pallas_call(
        sort_kernel,
        out_shape=(
            jax.ShapeDtypeStruct((8, LANES), jnp.int32),
            jax.ShapeDtypeStruct((LANES, LANES), jnp.bfloat16),
        ),
        in_specs=[pl.BlockSpec(memory_space=pltpu.SMEM)] + [vmem] * 3,
        out_specs=[vmem] * 2,
    )(count, query_row, target_device, target_row)


def compare_owner(n, stage, row, words, mains, tails, pay):
    sub = lax.broadcasted_iota(jnp.int32, (8, LANES), 0)
    lane = lax.broadcasted_iota(jnp.int32, (8, LANES), 1)
    choice = jnp.where(lane < 96, lane // MAIN, (lane - 96) // FRAMES)

    def pick(parts):
        return jnp.where(choice == 0, parts[0], jnp.where(choice == 1, parts[1], parts[2]))

    def operand(main, ends):
        end = jnp.concatenate([jnp.where(sub < 4, ends[0], pltpu.roll(ends[1], 4, 0)), ends[2]], axis=0)
        return main + [end.astype(jnp.bfloat16)]

    def half(h):
        query_main, query_ends, target_main, target_ends = [], [], [], []
        for t in range(3):
            slot = min(3 * h + t, SLOTS - 1)
            query = words[n, 0, slot]
            target = words[n, 1, slot]
            query_main.append(mains[(row * COLS + n) * CLIPS + query])
            query_ends.append(tails[(row * COLS + n) * CLIPS + query])
            target_main.append(mains[target])
            target_ends.append(tails[target])
        right = operand(target_main, target_ends) + [jnp.zeros((16, LANES), jnp.bfloat16)]
        product = lax.dot_general(
            jnp.concatenate(operand(query_main, query_ends), axis=0),
            jnp.concatenate(right, axis=0),
            (((1,), (1,)), ((), ())),
            preferred_element_type=jnp.float32,
        )
        main = [
            pick([product[t * MAIN + k * 8 : t * MAIN + k * 8 + 8] for t in range(3)])
            for k in range(4)
        ]
        front = product[96:104]
        end = pick([front, pltpu.roll(front, 4, 0), product[104:112]])
        return jnp.concatenate(main, axis=0).astype(jnp.bfloat16), end

    _, first, amount = STAGES[stage]
    for base in range(0, amount, 4):
        start = STARTS[stage] + base // 4 * QUAD
        several = min(4, amount - base)
        rows = []
        for b in range(0, several, 2):
            ends = []
            for k in (b, b + 1):
                pay[n, start + k * MAIN : start + (k + 1) * MAIN, :], end = half(first + base + k)
                ends.append(end)
            rows.append(jnp.where(sub < 4, ends[0], pltpu.roll(ends[1], 4, 0)))
        rows = jnp.concatenate([rows[0], rows[-1]], axis=0).astype(jnp.bfloat16)
        pay[n, start + several * MAIN : start + several * MAIN + 16, :] = rows


def chamfer(got, frames, first, stop):
    lane = lax.broadcasted_iota(jnp.int32, (8, LANES), 1)

    def best(x):
        top = jnp.maximum(x, shift(x, 4))
        top = jnp.maximum(top, shift(top, 8))
        top = jnp.maximum(top, shift(top, 16))
        ends = [shift(x, 96 + t * FRAMES - 32 * t) for t in range(3)]
        end = jnp.where(lane < 32, ends[0], jnp.where(lane < 64, ends[1], ends[2]))
        return jnp.maximum(top, end)

    def add(start, amount):
        total = got[0, pl.ds(start, amount), :].astype(jnp.float32)
        for m in range(1, SLICES):
            total += got[m, pl.ds(start, amount), :].astype(jnp.float32)
        return total

    def quad(q, amount):
        base = pl.multiple_of(q * QUAD, 16)
        ends = add(pl.multiple_of(base + amount * MAIN, 16), 16)
        for b in range(amount):
            total = add(pl.multiple_of(base + b * MAIN, 16), MAIN)
            main = [best(total[k * 8 : k * 8 + 8]) for k in range(4)]
            main = (main[0] + main[1]) + (main[2] + main[3])
            main = main + pltpu.roll(main, 4, 0)
            end = best(ends[b // 2 * 8 : b // 2 * 8 + 8])
            if b % 2:
                end = pltpu.roll(end, 4, 0)
            value = (main + end) * (1.0 / REGIONS)
            for f in range(FRAMES):
                frames[f, pl.ds(q * 4 + b, 1), :] = value[f : f + 1]

    if (stop - first) % 4:
        quad(first // 4, stop - first)
    else:

        def step(q, carry):
            quad(q, 4)
            return carry

        lax.fori_loop(first // 4, stop // 4, step, 0)


def convolve(padded, kernels):
    channels = padded.shape[3]
    rows = padded.shape[2]
    total = None
    for dy in range(3):
        wide = jnp.concatenate(
            [padded[dy : dy + 4, dx : dx + 4] for dx in range(3)], axis=-1
        ).reshape(16 * rows, 3 * channels)
        part = dot_split(wide, kernels[dy])
        total = part if total is None else total + part
    return total


def refine(frames, place, first, seconds, third, lasts, maps, scores, one, two):
    pairs = PAIRS
    ch1 = first.shape[1]
    ch2 = seconds.shape[1]
    taps = first[...].astype(jnp.float32)
    spread = []
    for i in range(FRAMES):
        value = frames[i]
        for j in range(FRAMES):
            spread.append(
                jnp.concatenate(
                    [
                        jnp.broadcast_to(value[:, 32 * t + j : 32 * t + j + 1], (24, ch1))
                        for t in range(3)
                    ],
                    axis=0,
                )
            )
    for i in range(FRAMES):
        for j in range(FRAMES):
            total = jnp.zeros((pairs, ch1), jnp.float32)
            for tap, pos in around(i, j):
                total += spread[pos] * taps[tap : tap + 1, :]
            one[1 + i, 1 + j] = jnp.maximum(total, 0.0)
    hidden = convolve(one, [seconds[dy * 3 * ch1 : (dy + 1) * 3 * ch1, :] for dy in range(3)])
    two[1:5, 1:5] = jnp.maximum(hidden, 0.0).reshape(4, 4, pairs, ch2)
    hidden = convolve(two, [third[dy * 3 * ch2 : (dy + 1) * 3 * ch2, :] for dy in range(3)])
    high, low = split(jnp.maximum(hidden, 0.0))
    nt = (((1,), (1,)), ((), ()))
    response = lax.dot_general(high, lasts[...], nt, preferred_element_type=jnp.float32)
    response += lax.dot_general(low, lasts[...], nt, preferred_element_type=jnp.float32)
    response = response.reshape(16, pairs, response.shape[1])
    tap_lane = lax.broadcasted_iota(jnp.int32, (pairs, response.shape[2]), 1)
    out_lane = lax.broadcasted_iota(jnp.int32, (pairs, LANES), 1)
    result = jnp.zeros((pairs, LANES), jnp.float32)
    for i in range(FRAMES):
        for j in range(FRAMES):
            total = jnp.zeros((pairs, response.shape[2]), jnp.float32)
            for tap, pos in around(i, j):
                total += jnp.where(tap_lane == tap, response[pos], 0.0)
            value = jnp.sum(total, axis=1, keepdims=True)
            result = jnp.where(out_lane == i * 4 + j, value, result)
    result = jnp.clip(result, -1.0, 1.0)
    top = jnp.maximum(result, shift(result, 1))
    top = jnp.maximum(top, shift(top, 2))
    kept = (out_lane < 16) & (lax.rem(out_lane, 4) == 0)
    score = jnp.sum(jnp.where(kept, top, 0.0), axis=1, keepdims=True) * (1.0 / FRAMES)
    result = jnp.where(out_lane == 16, score, result)
    result = jnp.concatenate([result, jnp.zeros((LANES - pairs, LANES), jnp.float32)], axis=0).T
    result = result[:24]
    high, low = split(result)
    rest = result - high.astype(jnp.float32) - low.astype(jnp.float32)
    result = sum(
        jnp.dot(part, place[...], preferred_element_type=jnp.float32)
        for part in (rest.astype(jnp.bfloat16), low, high)
    )
    maps[...] = result[:16, :SLOTS]
    scores[...] = result[16:17, :SLOTS]


def kernel(
    idx,
    place,
    features,
    first,
    second,
    third,
    last,
    maps,
    scores,
    feat,
    table,
    idx_all,
    words,
    units,
    scales,
    end_scales,
    mains,
    tails,
    pay,
    got,
    frames,
    one,
    two,
    seconds,
    lasts,
    a_send,
    a_recv,
    i_send,
    i_recv,
    b_send,
    b_recv,
    p_send,
    p_recv,
    own_sem,
    feat_sem,
):
    row = lax.axis_index("row")
    me = lax.axis_index("col")
    z = row // 2
    core = lax.rem(row, 2)
    my_y = me // 4
    my_x = lax.rem(me, 4)
    rows_z = lambda step: lax.rem(z + step, 4) * 2 + core
    rows_mate = lambda step: lax.rem(z + step, 4) * 2 + 1 - core
    mate = z * 2 + 1 - core
    offset = lambda i: lax.rem(7 * i, COLS)
    to = lambda i: lax.rem(my_y + offset(i) // 4, 4) * 4 + lax.rem(my_x + lax.rem(offset(i), 4), 4)
    source = lambda i: (
        lax.rem(my_y + 4 - offset(i) // 4, 4) * 4 + lax.rem(my_x + 4 - lax.rem(offset(i), 4), 4)
    )
    blocks = lambda r, c: table.at[pl.ds((r * COLS + c) * TILES, TILES)]
    load = lambda c: pltpu.make_async_copy(features.at[c], feat.at[c], feat_sem.at[c])
    measure, fill = make_units(load, feat, scales, end_scales)

    def loop(start, stop, body):
        def step(i, carry):
            body(i)
            return carry

        lax.fori_loop(start, stop, step, 0)

    loop(0, CLIPS, lambda c: load(c).start())
    barrier = pltpu.get_barrier_semaphore()

    def greet(device_row, device_col):
        pl.semaphore_signal(
            barrier, inc=1, device_id=(device_row, device_col), device_id_type=MESH
        )

    loop(1, COLS, lambda i: greet(row, to(i)))
    for other in (rows_z(1), rows_z(2), rows_z(3), mate):
        greet(other, me)

    def plane_copy(src, dst, send, recv, i, n):
        return pltpu.make_async_remote_copy(
            src_ref=src,
            dst_ref=dst,
            send_sem=send.at[i],
            recv_sem=recv.at[i],
            device_id=(row, n),
            device_id_type=MESH,
        )

    idx_copy = lambda i: plane_copy(idx, idx_all.at[me], i_send, i_recv, i, to(i))
    slice_copy = lambda i: plane_copy(units.at[to(i)], blocks(row, me), a_send, a_recv, i, to(i))
    slice_arrival = lambda i: plane_copy(
        units.at[0], blocks(row, source(i)), a_send, a_recv, i, to(i)
    )

    def part(buffer, n, stage):
        return buffer.at[n, pl.ds(STARTS[stage], SIZES[stage])]

    def part_copy(i, stage):
        return plane_copy(
            part(pay, to(i), stage),
            part(got, me, stage),
            p_send.at[stage],
            p_recv.at[stage],
            i,
            to(i),
        )

    def part_arrival(i, stage):
        return plane_copy(
            part(pay, 0, stage),
            part(got, source(i), stage),
            p_send.at[stage],
            p_recv.at[stage],
            i,
            to(i),
        )

    def own_part(stage):
        return pltpu.make_async_copy(
            part(pay, me, stage), part(got, me, stage), own_sem.at[1 + stage]
        )

    def forward(source_row, s, target_row, kind):
        return pltpu.make_async_remote_copy(
            src_ref=blocks(source_row, s),
            dst_ref=blocks(source_row, s),
            send_sem=b_send.at[kind, s],
            recv_sem=b_recv.at[kind, s],
            device_id=(target_row, me),
            device_id_type=MESH,
        )

    def spread(i):
        s = source(i)
        for step in (1, 3):
            forward(row, s, rows_z(step), step).start()
        forward(row, s, mate, 4).start()

    frames[...] = jnp.zeros_like(frames)
    one[...] = jnp.zeros_like(one)
    two[...] = jnp.zeros_like(two)
    seconds[...] = second[...].astype(jnp.float32).T.astype(jnp.bfloat16)
    ch3 = third.shape[1]
    lasts[...] = jnp.concatenate(
        [last[:, tap * ch3 : (tap + 1) * ch3].astype(jnp.float32) for tap in range(9)]
        + [jnp.zeros((7, ch3), jnp.float32)],
        axis=0,
    ).astype(jnp.bfloat16)
    measure()
    pl.semaphore_wait(barrier, COLS - 1 + 4)

    @pl.when(me < SLICES)
    def _():
        fill(blocks(row, me), me)
        spread(0)

    idx_all[me] = idx[...]
    loop(1, COLS, lambda i: idx_copy(i).start())

    def send_slice(i):
        n = to(i)

        @pl.when(n < SLICES)
        def _():
            fill(units.at[n], n)
            slice_copy(i).start()

    def pass_on(i):
        @pl.when(me < SLICES)
        def _():
            slice_arrival(i).wait_recv()
            spread(i)

    def send_and_pass(i):
        send_slice(i)
        pass_on(i - AHEAD)

    loop(1, AHEAD + 1, send_slice)
    loop(AHEAD + 1, COLS, send_and_pass)
    loop(COLS - AHEAD, COLS, pass_on)

    @pl.when(me < SLICES)
    def _():

        def relay(s):
            for step in (1, 3):
                block_row = rows_z(4 - step)
                forward(block_row, s, rows_z(step), step).wait_recv()

                @pl.when(lax.rem(s, 2) == step // 2)
                def _():
                    forward(block_row, s, rows_z(step), 2).start()

                forward(block_row, s, mate, 4 + step).start()

        loop(0, COLS, relay)

        def settle(s):
            forward(rows_mate(0), s, mate, 4).wait_recv()
            forward(rows_mate(3), s, mate, 5).wait_recv()
            forward(rows_mate(1), s, mate, 7).wait_recv()

        loop(0, COLS, settle)

    loop(1, COLS, lambda i: idx_copy(i).wait())

    @pl.when(me < SLICES)
    def _():
        local = pltpu.make_async_copy(idx_all, words, own_sem.at[0])
        local.start()

        def settle_block(block_row, s):
            i = block_row * COLS + s
            for c in range(CLIPS):
                mains[i * CLIPS + c] = table[i * TILES + c]
            for k in range(2):
                ends = table[i * TILES + CLIPS + k].astype(jnp.float32)
                for p in range(4):
                    pair = ends[p * 8 : p * 8 + 8]
                    tails[i * CLIPS + k * 8 + p * 2] = pair
                    tails[i * CLIPS + k * 8 + p * 2 + 1] = pltpu.roll(pair, 4, 0)

        def settle_near(k):
            step = k // 32
            block_row = lax.rem(z + step + step // 2, 4) * 2 + lax.rem(k // COLS, 2)
            settle_block(block_row, lax.rem(k, COLS))

        loop(0, 6 * COLS, settle_near)
        local.wait()
        begin = 0
        for stage, (stop, _, amount) in enumerate(STAGES):

            def relay_far(s):
                forward(rows_z(2), s, rows_z(1), 2).wait_recv()
                forward(rows_z(2), s, mate, 6).start()

            def settle_far(s):
                forward(rows_mate(2), s, mate, 6).wait_recv()
                settle_block(rows_z(2), s)
                settle_block(rows_mate(2), s)

            if stop > begin:
                loop(begin, stop, relay_far)
                loop(begin, stop, settle_far)
            begin = stop

            several = max(1, 8 // amount)

            def send_parts(step, stage=stage, several=several):
                some = [1 + step * several + k for k in range(several)]
                for i in some:
                    compare_owner(to(i), stage, row, words, mains, tails, pay)
                for i in some:

                    @pl.when(i < COLS)
                    def _(i=i):
                        part_copy(i, stage).start()

            loop(0, COLS // several, send_parts)
            own_part(stage).start()

    for stage, (_, first_group, amount) in enumerate(STAGES):

        def take_part(i, stage=stage):
            @pl.when(source(i) < SLICES)
            def _():
                part_arrival(i, stage).wait_recv()

        loop(1, COLS, take_part)

        @pl.when(me < SLICES)
        def _(stage=stage):
            own_part(stage).wait()

        chamfer(got, frames, first_group, first_group + amount)
    refine(frames, place, first, seconds, third, lasts, maps, scores, one, two)

    def drain_slice(i):
        @pl.when(to(i) < SLICES)
        def _():
            slice_copy(i).wait_send()

    loop(1, COLS, drain_slice)

    @pl.when(me < SLICES)
    def _():
        for stage in range(len(STAGES)):
            loop(1, COLS, lambda i, stage=stage: part_copy(i, stage).wait_send())

        def drain(s):
            forward(row, s, mate, 4).wait_send()
            for step in (1, 3):
                block_row = rows_z(4 - step)
                forward(row, s, rows_z(step), step).wait_send()
                forward(block_row, s, mate, 4 + step).wait_send()

                @pl.when(lax.rem(s, 2) == step // 2)
                def _():
                    forward(block_row, s, rows_z(step), 2).wait_send()

            forward(rows_z(2), s, mate, 6).wait_send()

        loop(0, COLS, drain)


def per_device(
    features,
    query_row,
    target_device,
    target_row,
    pair_count,
    conv_first,
    conv_second,
    conv_third,
    conv_last,
):
    idx, place = sort_slots(
        pair_count,
        query_row.reshape(1, SLOTS),
        target_device.reshape(1, SLOTS),
        target_row.reshape(1, SLOTS),
    )
    vmem = pl.BlockSpec(memory_space=pltpu.VMEM)
    dma = pltpu.SemaphoreType.DMA
    bf16, f32, i32 = jnp.bfloat16, jnp.float32, jnp.int32
    maps, scores = pl.pallas_call(
        kernel,
        out_shape=(
            jax.ShapeDtypeStruct((FRAMES * FRAMES, SLOTS), f32),
            jax.ShapeDtypeStruct((1, SLOTS), f32),
        ),
        in_specs=[vmem] * 2 + [pl.BlockSpec(memory_space=pl.ANY)] + [vmem] * 4,
        out_specs=[vmem] * 2,
        scratch_shapes=[
            pltpu.VMEM((CLIPS, REGIONS, FRAMES, DIM), f32),
            pltpu.VMEM((ROWS * COLS * TILES, MAIN, LANES), bf16),
            pltpu.VMEM((COLS, 8, LANES), i32),
            pltpu.SMEM((COLS, 8, LANES), i32),
            pltpu.VMEM((SLICES, TILES, MAIN, LANES), bf16),
            pltpu.VMEM((CLIPS, MAIN, LANES), f32),
            pltpu.VMEM((CLIPS // 4, 16, LANES), f32),
            pltpu.VMEM((ROWS * COLS * CLIPS, MAIN, LANES), bf16),
            pltpu.VMEM((ROWS * COLS * CLIPS, 8, LANES), f32),
            pltpu.VMEM((COLS, PAY, LANES), bf16),
            pltpu.VMEM((COLS, PAY, LANES), bf16),
            pltpu.VMEM((FRAMES, 24, LANES), f32),
            pltpu.VMEM((6, 6, 72, conv_first.shape[1]), f32),
            pltpu.VMEM((6, 6, 72, conv_second.shape[1]), f32),
            pltpu.VMEM(conv_second.shape, bf16),
            pltpu.VMEM((16, conv_third.shape[1]), bf16),
            dma((COLS,)),
            dma((COLS,)),
            dma((COLS,)),
            dma((COLS,)),
            dma((8, COLS)),
            dma((8, COLS)),
            dma((len(STAGES), COLS)),
            dma((len(STAGES), COLS)),
            dma((1 + len(STAGES),)),
            dma((CLIPS,)),
        ],
        compiler_params=pltpu.CompilerParams(
            collective_id=0, has_side_effects=True, vmem_limit_bytes=VMEM_LIMIT
        ),
    )(
        idx,
        place,
        features.transpose(0, 2, 1, 3),
        conv_first,
        conv_second.T,
        conv_third,
        conv_last.T,
    )
    return maps.T, scores[0]


def solution(mesh):
    return jax.shard_map(
        per_device,
        mesh=mesh,
        in_specs=(
            P(("row", "col"), None, None, None),
            P(("row", "col")),
            P(("row", "col"), None),
            P(("row", "col")),
            P(("row", "col")),
            P(),
            P(),
            P(),
            P(),
        ),
        out_specs=(P(("row", "col"), None), P(("row", "col"))),
        check_vma=False,
    )
```
